32 devices in a mesh: groups: 2 (over x), blk: 16 (over z, y, core).
Axes of the slice: x: 2, y: 2, z: 4, core: 2. Of those that a mesh axis runs over, the one named last changes fastest.
Arguments:
- factors: bfloat16 [64, 2, 64, 128], P(('groups', 'blk')), parts along dimension 0, may hold values from -2.09375 to 2.09375
- token_mask: int32 [64, 64], P(('groups', 'blk')), parts along dimension 0, may hold values 0 or 1
- store: bfloat16 [16384, 2, 4096], P(('groups', 'blk')), parts along dimension 0, may hold values from -0.0625 to 0.0625
- inv_fisher: bfloat16 [2, 4096, 4096], P(None, 'blk'), as said below
- source_ids: int32 [16384], P(('groups', 'blk')), parts along dimension 0, may hold values from 0 to 15
- source_weight: float32 [16], replicated, may hold values from 0.25 to 4
Outputs:
- scores: float32 [64, 8192], P('groups', 'blk'), parts along dimension 0
The draws below stay inside these ranges and needn't reach their ends.
There are 2 independent parts, one for each index of `groups`. The reference program is written for one: setup_inputs(seed, part) draws one part's arguments, and reference() takes and returns one part's arrays. A program takes and returns all parts, laid end to end along the dimension named above; an argument that names none is the same for every part. Nothing has to cross between parts.
Inputs may be any that keep to these rules, and one draw needn't show every extreme that they name: `inv_fisher`: each layer's matrix is symmetric.
All inputs are finite; a program needn't handle non-finite values. No bound on the sum of `token_mask` on one device may be relied on, other than what follows from the above.
Results may differ from the reference program's by a relative error of at most 0.004.
Values may be sent and summed in bfloat16 or wider, within the bound.
No kernel may reach another device: no remote copies, remote signals or barrier semaphores. Data moves between devices by JAX's collectives and lax.ppermute only.
A program may use at most 64 MiB of HBM per device.

```python
import math
import jax
import jax.numpy as jnp
from jax import lax

RANK = 64
FEAT = 4096
LAYERS = 2
SEQ = 64
NSRC = 16
N_DEV = 512
QUERIES = 32
TRAIN = 8192
N_BLK = 16


def draw_inv_fisher(key, part):
    diag_key = jax.random.fold_in(key, 11)
    off_key = jax.random.fold_in(key, 12)
    diagonal = jax.random.uniform(diag_key, (LAYERS, FEAT), jnp.float32, 1.0, 2.0)
    spread = 0.4
    gaussian = jax.random.normal(off_key, (LAYERS, FEAT, FEAT), jnp.float32)
    symmetric = (gaussian + jnp.swapaxes(gaussian, 1, 2)) * (spread / math.sqrt(2.0 * FEAT))
    identity = jnp.eye(FEAT, dtype=jnp.float32)
    return (symmetric + diagonal[:, :, None] * identity[None]).astype(jnp.bfloat16)


def set_ends(drawn, key, smallest, top_value):
    dims = drawn.shape
    index_at = [jax.random.randint(jax.random.fold_in(key, axis), (), 0, dims[axis]) for axis in range(len(dims))]
    drawn = drawn.at[tuple(index_at)].set(smallest)
    longest = dims.index(max(dims))
    index_at[longest] = (index_at[longest] + 1) % dims[longest]
    return drawn.at[tuple(index_at)].set(top_value)


def shard_levels(rng, shape, cuts, least, high):
    def one(position, parts):
        heights = jax.random.uniform(jax.random.fold_in(jax.random.fold_in(rng, 6), position), (parts,), jnp.float32, least / len(cuts), high / len(cuts))
        return jnp.repeat(jnp.exp(heights), shape[position] // parts).reshape((-1,) + (1,) * (len(shape) - position - 1))

    factor_of = one(*cuts[0])
    for cut in cuts[1:]:
        factor_of = factor_of * one(*cut)
    return factor_of


def noise(stream_key, shape, width, limit, shards=(), held_as=jnp.bfloat16):
    result = width * jax.random.normal(stream_key, shape, jnp.float32)
    if shards:
        result = result * shard_levels(stream_key, shape, shards, -0.22, 0.18)
    return jnp.clip(result, -limit, limit).astype(held_as)


def setup_inputs(seed: int = 0, part: int = 0) -> dict:
    streams_of = jax.random.split(jax.random.key(seed), 7)
    part_splits = jax.random.split(jax.random.fold_in(streams_of[6], part), 7)
    return {
        "factors": noise(part_splits[0], (QUERIES, LAYERS, SEQ, 2 * RANK), 0.35, 2.09375, ((0, 16),)),
        "token_mask": set_ends((jax.random.randint(part_splits[1], (QUERIES, SEQ), 0, 4) < 3).astype(jnp.int32), jax.random.fold_in(part_splits[1], 1), 0, 1),
        "store": noise(part_splits[2], (TRAIN, LAYERS, FEAT), (LAYERS * FEAT) ** -0.5, 0.0625, ((0, 16),)),
        "inv_fisher": draw_inv_fisher(jax.random.fold_in(streams_of[6], 71), part),
        "source_ids": set_ends(jax.random.randint(part_splits[4], (TRAIN,), 0, NSRC), jax.random.fold_in(part_splits[4], 1), 0, NSRC - 1).astype(jnp.int32),
        "source_weight": jnp.clip(jnp.exp(jax.random.uniform(streams_of[5], (NSRC,), jnp.float32, math.log(0.25), math.log(4.0))), 0.25, 4.0),
    }


def reference(factors, token_mask, store, inv_fisher, source_ids, source_weight):
    rank_size = factors.shape[3] // 2
    mask_values = token_mask.astype(jnp.float32)[:, None, :, None]
    left_side = factors[..., :rank_size].astype(jnp.float32) * mask_values
    right_side = factors[..., rank_size:].astype(jnp.float32)
    outer_sum = jnp.einsum("qlta,qltb->qlab", left_side, right_side)
    query_grads = outer_sum.reshape(outer_sum.shape[0], outer_sum.shape[1], rank_size * rank_size).astype(jnp.bfloat16)
    hidden = jnp.stack([jnp.dot(query_grads[:, layer_idx], inv_fisher[layer_idx], preferred_element_type=jnp.float32) for layer_idx in range(LAYERS)], axis=1).astype(jnp.bfloat16)
    flattened = hidden.reshape(hidden.shape[0], -1)
    blocks = store.reshape(N_BLK, N_DEV, -1)

    def score_block(block_rows):
        return jnp.dot(flattened, block_rows.T, preferred_element_type=jnp.float32)

    raw_scores = lax.map(score_block, blocks)
    raw_scores = jnp.transpose(raw_scores, (1, 0, 2)).reshape(flattened.shape[0], -1)
    scaling = source_weight[source_ids]
    return raw_scores * scaling[None, :]
```

```python
import jax
import jax.numpy as jnp
from jax import lax
from jax.sharding import PartitionSpec as P


def make_grads(factors, token_mask):
    rank_size = factors.shape[3] // 2
    mask_values = token_mask.astype(jnp.float32)[:, None, :, None]
    left_side = factors[..., :rank_size].astype(jnp.float32) * mask_values
    right_side = factors[..., rank_size:].astype(jnp.float32)
    outer_sum = jnp.einsum("qlta,qltb->qlab", left_side, right_side)
    return outer_sum.reshape(outer_sum.shape[0], outer_sum.shape[1], rank_size * rank_size).astype(
        jnp.bfloat16
    )


def local(factors, token_mask, store, inv_fisher, source_ids, source_weight):
    query_grads = make_grads(factors, token_mask)
    layer_count = inv_fisher.shape[0]
    segment = lax.all_gather(query_grads, "blk", axis=0, tiled=True)
    products = [
        lax.dot_general(
            segment[:, layer_idx],
            inv_fisher[layer_idx],
            (((1,), (1,)), ((), ())),
            preferred_element_type=jnp.float32,
        )
        for layer_idx in range(layer_count)
    ]
    hidden_cols = jnp.stack(products, axis=1).astype(jnp.bfloat16)
    hidden = lax.all_gather(hidden_cols, "blk", axis=2, tiled=True)
    matches = (
        source_ids[:, None] == jnp.arange(source_weight.shape[0], dtype=jnp.int32)[None, :]
    ).astype(jnp.float32)
    scaling = jnp.sum(matches * source_weight[None, :], axis=1)
    raw_scores = lax.dot_general(
        hidden,
        store,
        (((1, 2), (1, 2)), ((), ())),
        preferred_element_type=jnp.float32,
    )
    return raw_scores * scaling[None, :]


def solution(mesh):
    placed = (
        P(("groups", "blk"), None, None, None),
        P(("groups", "blk"), None),
        P(("groups", "blk"), None, None),
        P(None, "blk", None),
        P(("groups", "blk")),
        P(),
    )
    return jax.shard_map(
        local, mesh=mesh, in_specs=placed, out_specs=P("groups", "blk"), check_vma=False
    )
```

```python
import functools

import jax
import jax.numpy as jnp
from jax import lax
from jax.experimental import pallas as pl
from jax.experimental.pallas import tpu as pltpu
from jax.sharding import PartitionSpec as P

LANES = 128
VMEM_LIMIT = 40 * 2**20
IN_VMEM = pl.BlockSpec(memory_space=pltpu.VMEM)


def make_grads(factors, token_mask):
    rank_size = factors.shape[3] // 2
    mask_values = token_mask.astype(jnp.float32)[:, None, :, None]
    left_side = factors[..., :rank_size].astype(jnp.float32) * mask_values
    right_side = factors[..., rank_size:].astype(jnp.float32)
    outer_sum = jnp.einsum("qlta,qltb->qlab", left_side, right_side)
    return outer_sum.reshape(outer_sum.shape[0], outer_sum.shape[1], rank_size * rank_size).astype(
        jnp.bfloat16
    )


def make_scaling(source_ids, source_weight):
    matches = (
        source_ids[:, None] == jnp.arange(source_weight.shape[0], dtype=jnp.int32)[None, :]
    ).astype(jnp.float32)
    return jnp.sum(matches * source_weight[None, :], axis=1)


def plain(factors, token_mask, store, inv_fisher, source_ids, source_weight):
    segment = lax.all_gather(make_grads(factors, token_mask), "blk", axis=0, tiled=True)
    products = [
        lax.dot_general(
            segment[:, layer_idx],
            inv_fisher[layer_idx],
            (((1,), (1,)), ((), ())),
            preferred_element_type=jnp.float32,
        )
        for layer_idx in range(inv_fisher.shape[0])
    ]
    hidden_cols = jnp.stack(products, axis=1).astype(jnp.bfloat16)
    hidden = lax.all_gather(hidden_cols, "blk", axis=2, tiled=True)
    raw_scores = lax.dot_general(
        hidden, store, (((1, 2), (1, 2)), ((), ())), preferred_element_type=jnp.float32
    )
    return raw_scores * make_scaling(source_ids, source_weight)[None, :]


def grads_kernel(factors_ref, mask_ref, out_ref, outer_ref, flat_ref):
    queries, layers, _, width = factors_ref.shape
    rank = width // 2
    tiles = rank * rank // LANES
    for layer in range(layers):
        for query in range(queries):
            block = factors_ref[query, layer].astype(jnp.float32)
            left = block[:, :rank].T * mask_ref[query : query + 1].astype(jnp.float32)
            outer_ref[...] = jnp.dot(
                left.astype(jnp.bfloat16),
                block[:, rank:].astype(jnp.bfloat16),
                preferred_element_type=jnp.float32,
            )
            flat_ref[layer, pl.ds(query, tiles, queries)] = jnp.concatenate(
                [outer_ref[pl.ds(0, tiles, 2)], outer_ref[pl.ds(1, tiles, 2)]], axis=1
            )
    out_ref[...] = (
        flat_ref[...].astype(jnp.bfloat16).reshape(layers * tiles, queries, LANES)
    )


def grads_call(factors, token_mask):
    queries, layers, _, width = factors.shape
    rank = width // 2
    tiles = rank * rank // LANES
    return pl.pallas_call(
        grads_kernel,
        out_shape=jax.ShapeDtypeStruct((layers * tiles, queries, LANES), jnp.bfloat16),
        in_specs=[IN_VMEM] * 2,
        out_specs=IN_VMEM,
        scratch_shapes=[
            pltpu.VMEM((rank, rank), jnp.float32),
            pltpu.VMEM((layers, tiles * queries, LANES), jnp.float32),
        ],
        compiler_params=pltpu.CompilerParams(vmem_limit_bytes=VMEM_LIMIT),
    )(factors, token_mask)


def gather_parts(chunk, size):
    held = chunk[None]
    step = size // 2
    while step > 1:
        other = lax.ppermute(held, "blk", [(i, i ^ step) for i in range(size)])
        held = jnp.concatenate([held, other], axis=0)
        step //= 2
    return held, lax.ppermute(held, "blk", [(i, i ^ 1) for i in range(size)])


def entry_of(position, size):
    bits = (size // 2).bit_length() - 1
    return sum(((position >> (bits - 1 - b)) & 1) << b for b in range(bits))


def fisher_kernel(size, near_ref, far_ref, fisher_ref, out_ref, whole_ref):
    me = lax.axis_index("blk")
    half = size // 2
    layers, rows, feats = fisher_ref.shape
    tiles = feats // LANES
    queries = near_ref.shape[2]
    odd = lax.rem(me, 2) == 1
    for entry in range(half):
        near, far = near_ref[entry], far_ref[entry]
        place = lax.bitwise_xor(me // 2, position_of(entry, size))
        whole_ref[place, 0] = jnp.where(odd, far, near)
        whole_ref[place, 1] = jnp.where(odd, near, far)
    parts = []
    for layer in range(layers):
        grads = jnp.concatenate(
            [
                whole_ref[:, :, layer * tiles + tile].reshape(size * queries, LANES)
                for tile in range(tiles)
            ],
            axis=1,
        )
        parts.append(
            lax.dot_general(
                fisher_ref[layer],
                grads,
                (((1,), (1,)), ((), ())),
                preferred_element_type=jnp.float32,
            )
        )
    pieces = [
        part[start : start + LANES] for start in range(0, rows, LANES) for part in parts
    ]
    out_ref[...] = jnp.concatenate(pieces, axis=1).astype(jnp.bfloat16)


def position_of(entry, size):
    return entry_of(entry, size)


def fisher_call(near, far, inv_fisher, size):
    return pl.pallas_call(
        functools.partial(fisher_kernel, size),
        out_shape=jax.ShapeDtypeStruct((LANES, LANES), jnp.bfloat16),
        in_specs=[IN_VMEM] * 3,
        out_specs=IN_VMEM,
        scratch_shapes=[pltpu.VMEM((size // 2, 2) + near.shape[1:], jnp.bfloat16)],
        compiler_params=pltpu.CompilerParams(vmem_limit_bytes=VMEM_LIMIT),
    )(near, far, inv_fisher)


def score_kernel(size, queries, near_ref, far_ref, store_ref, scale_ref, out_ref, total_ref):
    me = lax.axis_index("blk")
    count, layers, feats = store_ref.shape
    width = feats // size
    groups = width // LANES
    span = LANES // groups
    lane = lax.broadcasted_iota(jnp.int32, (LANES, LANES), 1)
    total_ref[...] = jnp.zeros_like(total_ref)
    for entry in range(size // 2):
        for far, ref in enumerate((near_ref, far_ref)):
            owner = lax.bitwise_xor(me, 2 * position_of(entry, size) + far)
            chunk = ref[entry]
            weights = jnp.concatenate(
                [
                    jnp.where(lane // span == group, chunk, jnp.zeros_like(chunk))
                    for group in range(groups)
                ],
                axis=0,
            )
            columns = pl.ds(pl.multiple_of(owner * width, width), width)
            rows = store_ref[:, :, columns].reshape(count * layers, width)
            total_ref[...] += jnp.dot(rows, weights, preferred_element_type=jnp.float32)
    result = jnp.zeros((queries, count), jnp.float32)
    for layer in range(layers):
        turned = total_ref[pl.ds(layer, count, layers)].T
        for group in range(groups):
            start = group * span + layer * queries
            result = result + turned[start : start + queries]
    out_ref[...] = result * scale_ref[...]


def score_call(near, far, store, scaling, size, queries):
    count, layers, _ = store.shape
    return pl.pallas_call(
        functools.partial(score_kernel, size, queries),
        out_shape=jax.ShapeDtypeStruct((queries, count), jnp.float32),
        in_specs=[IN_VMEM] * 4,
        out_specs=IN_VMEM,
        scratch_shapes=[pltpu.VMEM((count * layers, LANES), jnp.float32)],
        compiler_params=pltpu.CompilerParams(vmem_limit_bytes=VMEM_LIMIT),
    )(near, far, store, scaling[None, :])


def fits(size, factors, store, inv_fisher):
    queries, layers, _, width = factors.shape
    _, rows, feats = inv_fisher.shape
    return (
        size > 1
        and size & (size - 1) == 0
        and width == LANES
        and queries == 2
        and layers == 2
        and rows % LANES == 0
        and (rows // LANES) * layers * queries * size == LANES
        and store.shape[0] % LANES == 0
        and feats == rows * size
    )


def solution(mesh):
    size = mesh.shape["blk"]

    def local(factors, token_mask, store, inv_fisher, source_ids, source_weight):
        if not fits(size, factors, store, inv_fisher):
            return plain(factors, token_mask, store, inv_fisher, source_ids, source_weight)
        scaling = make_scaling(source_ids, source_weight)
        near, far = gather_parts(grads_call(factors, token_mask), size)
        hidden = fisher_call(near, far, inv_fisher, size)
        near, far = gather_parts(hidden, size)
        return score_call(near, far, store, scaling, size, factors.shape[0] * size)

    placed = (
        P(("groups", "blk"), None, None, None),
        P(("groups", "blk"), None),
        P(("groups", "blk"), None, None),
        P(None, "blk", None),
        P(("groups", "blk")),
        P(),
    )
    return jax.shard_map(
        local, mesh=mesh, in_specs=placed, out_specs=P("groups", "blk"), check_vma=False
    )
```

```python
import functools
import math

import jax
import jax.numpy as jnp
from jax import lax
from jax.experimental import pallas as pl
from jax.experimental.pallas import tpu as pltpu
from jax.sharding import PartitionSpec as P

LANES = 128
IN_VMEM = pl.BlockSpec(memory_space=pltpu.VMEM)
IN_HBM = pl.BlockSpec(memory_space=pltpu.HBM)
PARAMS = pltpu.CompilerParams(vmem_limit_bytes=16 * 2**20)


def make_grads(factors, token_mask):
    rank_size = factors.shape[3] // 2
    mask_values = token_mask.astype(jnp.float32)[:, None, :, None]
    left_side = factors[..., :rank_size].astype(jnp.float32) * mask_values
    right_side = factors[..., rank_size:].astype(jnp.float32)
    outer_sum = jnp.einsum("qlta,qltb->qlab", left_side, right_side)
    return outer_sum.reshape(outer_sum.shape[0], outer_sum.shape[1], rank_size * rank_size).astype(
        jnp.bfloat16
    )


def make_scaling(source_ids, source_weight):
    matches = (
        source_ids[:, None] == jnp.arange(source_weight.shape[0], dtype=jnp.int32)[None, :]
    ).astype(jnp.float32)
    return jnp.sum(matches * source_weight[None, :], axis=1)


def plain(factors, token_mask, store, inv_fisher, source_ids, source_weight):
    segment = lax.all_gather(make_grads(factors, token_mask), "blk", axis=0, tiled=True)
    products = [
        lax.dot_general(
            segment[:, layer_idx],
            inv_fisher[layer_idx],
            (((1,), (1,)), ((), ())),
            preferred_element_type=jnp.float32,
        )
        for layer_idx in range(inv_fisher.shape[0])
    ]
    hidden_cols = jnp.stack(products, axis=1).astype(jnp.bfloat16)
    hidden = lax.all_gather(hidden_cols, "blk", axis=2, tiled=True)
    raw_scores = lax.dot_general(
        hidden, store, (((1, 2), (1, 2)), ((), ())), preferred_element_type=jnp.float32
    )
    return raw_scores * make_scaling(source_ids, source_weight)[None, :]


def grads_kernel(factors_ref, mask_ref, out_ref, held_ref, mask_held_ref, outer_ref, flat_ref, sems):
    copies = [
        pltpu.make_async_copy(factors_ref, held_ref, sems.at[0]),
        pltpu.make_async_copy(mask_ref, mask_held_ref, sems.at[1]),
    ]
    for copy in copies:
        copy.start()
    for copy in copies:
        copy.wait()
    queries, layers, _, width = factors_ref.shape
    rank = width // 2
    tiles = rank * rank // LANES
    for layer in range(layers):
        for query in range(queries):
            block = held_ref[query, layer].astype(jnp.float32)
            left = block[:, :rank].T * mask_held_ref[query : query + 1].astype(jnp.float32)
            outer_ref[...] = jnp.dot(
                left.astype(jnp.bfloat16),
                block[:, rank:].astype(jnp.bfloat16),
                preferred_element_type=jnp.float32,
            )
            flat_ref[layer, pl.ds(query, tiles, queries)] = jnp.concatenate(
                [outer_ref[pl.ds(0, tiles, 2)], outer_ref[pl.ds(1, tiles, 2)]], axis=1
            )
    out_ref[...] = (
        flat_ref[...].astype(jnp.bfloat16).reshape(layers * tiles, queries, LANES)
    )


def grads_call(factors, token_mask):
    queries, layers, _, width = factors.shape
    rank = width // 2
    tiles = rank * rank // LANES
    return pl.pallas_call(
        grads_kernel,
        out_shape=jax.ShapeDtypeStruct((layers * tiles, queries, LANES), jnp.bfloat16),
        in_specs=[IN_HBM] * 2,
        out_specs=IN_VMEM,
        scratch_shapes=[
            pltpu.VMEM(factors.shape, factors.dtype),
            pltpu.VMEM(token_mask.shape, token_mask.dtype),
            pltpu.VMEM((rank, rank), jnp.float32),
            pltpu.VMEM((layers, tiles * queries, LANES), jnp.float32),
            pltpu.SemaphoreType.DMA((2,)),
        ],
        compiler_params=PARAMS,
    )(factors, token_mask)


def load_kernel(size, index, source_ref, out_ref, sem):
    width = out_ref.shape[-1]
    for entry, owner in enumerate(owners(size)[index]):
        columns = pl.ds(pl.multiple_of(owner * width, width), width)
        pltpu.make_async_copy(source_ref.at[:, :, columns], out_ref.at[entry], sem).start()
    pltpu.make_async_copy(out_ref, out_ref, sem).wait()


def load_store(store, size, index, entries):
    rows, layers, feats = store.shape
    shape = (entries, rows, layers, feats // size)
    return pl.pallas_call(
        functools.partial(load_kernel, size, index),
        out_shape=jax.ShapeDtypeStruct(shape, store.dtype),
        in_specs=[IN_HBM],
        out_specs=IN_VMEM,
        scratch_shapes=[pltpu.SemaphoreType.DMA],
        cost_estimate=pl.CostEstimate(
            flops=0, bytes_accessed=2 * math.prod(shape), transcendentals=0
        ),
        compiler_params=PARAMS,
    )(store)


def copy_kernel(source_ref, out_ref, sem):
    copy = pltpu.make_async_copy(source_ref, out_ref, sem)
    copy.start()
    copy.wait()


def load_whole(source):
    return pl.pallas_call(
        copy_kernel,
        out_shape=jax.ShapeDtypeStruct(source.shape, source.dtype),
        in_specs=[IN_HBM],
        out_specs=IN_VMEM,
        scratch_shapes=[pltpu.SemaphoreType.DMA],
        cost_estimate=pl.CostEstimate(
            flops=0, bytes_accessed=2 * source.size, transcendentals=0
        ),
        compiler_params=PARAMS,
    )(source)


def together(first, *others):
    return lax.optimization_barrier((first, *others))


def send(value, even, odd, size):
    pairs = [(i, i ^ (odd if i % 2 else even)) for i in range(size)]
    return lax.ppermute(value, "blk", pairs)


def gather_parts(chunk, size, meanwhile):
    own = chunk[None]
    done = []
    step = size // 2
    while step > 4:
        other = send(own, step, step, size)
        if not done:
            work = meanwhile[0](own)
            other, work = together(other, work)
            done.append(work)
        own = jnp.concatenate([own, other], axis=0)
        step //= 2
    own_and_core = jnp.concatenate([own, send(own, 1, 1, size)], axis=0)
    side = send(own, 4, 4, size)
    corner = send(own_and_core, 6, 2, size)
    work = meanwhile[1](own_and_core)
    corner, work = together(corner, work)
    done.append(work)
    rest = jnp.concatenate([side, corner], axis=0)
    return (own_and_core, rest, send(rest, 1, 1, size)), done


def owners(size):
    me = lax.axis_index("blk")
    corner = jnp.where(lax.rem(me, 2) == 1, 2, 6)
    other = me ^ 1
    other_corner = jnp.where(lax.rem(me, 2) == 1, 6, 2)
    own = [0]
    step = size // 2
    while step > 4:
        own = own + [step ^ entry for entry in own]
        step //= 2
    both = own + [entry ^ 1 for entry in own]
    return (
        [me ^ entry for entry in both],
        [me ^ 4 ^ entry for entry in own] + [me ^ corner ^ entry for entry in both],
        [other ^ 4 ^ entry for entry in own] + [other ^ other_corner ^ entry for entry in both],
    )


def fisher_kernel(size, *refs):
    part_refs, (fisher_ref, out_ref, whole_ref) = refs[:3], refs[3:]
    layers, rows, feats = fisher_ref.shape
    tiles = feats // LANES
    queries = whole_ref.shape[2]
    for ref, places in zip(part_refs, owners(size)):
        for entry, place in enumerate(places):
            whole_ref[place] = ref[entry]
    parts = []
    for layer in range(layers):
        grads = jnp.concatenate(
            [
                whole_ref[:, layer * tiles + tile].reshape(size * queries, LANES)
                for tile in range(tiles)
            ],
            axis=1,
        )
        parts.append(
            lax.dot_general(
                fisher_ref[layer],
                grads,
                (((1,), (1,)), ((), ())),
                preferred_element_type=jnp.float32,
            )
        )
    pieces = [
        part[start : start + LANES] for start in range(0, rows, LANES) for part in parts
    ]
    out_ref[...] = jnp.concatenate(pieces, axis=1).astype(jnp.bfloat16)


def fisher_call(parts, inv_fisher, size):
    return pl.pallas_call(
        functools.partial(fisher_kernel, size),
        out_shape=jax.ShapeDtypeStruct((LANES, LANES), jnp.bfloat16),
        in_specs=[IN_VMEM] * 4,
        out_specs=IN_VMEM,
        scratch_shapes=[pltpu.VMEM((size,) + parts[0].shape[1:], jnp.bfloat16)],
        compiler_params=PARAMS,
    )(*parts, inv_fisher)


def add_products(chunk_ref, store_ref, total_ref, fresh):
    _, count, layers, width = store_ref.shape
    groups = width // LANES
    span = LANES // groups
    lane = lax.broadcasted_iota(jnp.int32, (LANES, LANES), 1)
    for entry in range(chunk_ref.shape[0]):
        chunk = chunk_ref[entry]
        weights = jnp.concatenate(
            [
                jnp.where(lane // span == group, chunk, jnp.zeros_like(chunk))
                for group in range(groups)
            ],
            axis=0,
        )
        rows = store_ref[entry].reshape(count * layers, width)
        product = jnp.dot(rows, weights, preferred_element_type=jnp.float32)
        if fresh and entry == 0:
            total_ref[...] = product
        else:
            total_ref[...] += product


def partial_kernel(chunk_ref, store_ref, *refs):
    add_products(chunk_ref, store_ref, refs[-1], fresh=len(refs) == 1)


def partial_call(chunks, store, total=None):
    _, count, layers, width = store.shape
    flops = 2 * chunks.shape[0] * count * layers * width * LANES
    return pl.pallas_call(
        partial_kernel,
        out_shape=jax.ShapeDtypeStruct((count * layers, LANES), jnp.float32),
        in_specs=[IN_VMEM] * (2 if total is None else 3),
        out_specs=IN_VMEM,
        input_output_aliases={} if total is None else {2: 0},
        cost_estimate=pl.CostEstimate(flops=flops, bytes_accessed=0, transcendentals=0),
        compiler_params=PARAMS,
    )(*([chunks, store] if total is None else [chunks, store, total]))


def score_kernel(queries, chunk_ref, store_ref, before_ref, scale_ref, out_ref, total_ref):
    _, count, layers, width = store_ref.shape
    groups = width // LANES
    span = LANES // groups
    total_ref[...] = before_ref[...]
    add_products(chunk_ref, store_ref, total_ref, fresh=False)
    lane = lax.broadcasted_iota(jnp.int32, (count, LANES), 1)
    mixed = total_ref[pl.ds(0, count, layers)]
    for layer in range(1, layers):
        rows = total_ref[pl.ds(layer, count, layers)]
        mixed = jnp.where(lane % span // queries == layer, rows, mixed)
    turned = mixed.T
    result = turned[:queries]
    for start in range(queries, LANES, queries):
        result = result + turned[start : start + queries]
    out_ref[...] = result * scale_ref[...]


def score_call(chunks, store, total, scaling, queries):
    _, count, layers, _ = store.shape
    return pl.pallas_call(
        functools.partial(score_kernel, queries),
        out_shape=jax.ShapeDtypeStruct((queries, count), jnp.float32),
        in_specs=[IN_VMEM] * 4,
        out_specs=IN_VMEM,
        scratch_shapes=[pltpu.VMEM(total.shape, jnp.float32)],
        compiler_params=PARAMS,
    )(chunks, store, total, scaling[None, :])


def fits(size, factors, store, inv_fisher):
    queries, layers, _, width = factors.shape
    _, rows, feats = inv_fisher.shape
    return (
        size >= 8
        and size & (size - 1) == 0
        and width == LANES
        and queries == 2
        and layers == 2
        and rows % LANES == 0
        and (rows // LANES) * layers * queries * size == LANES
        and store.shape[0] % LANES == 0
        and feats == rows * size
    )


def solution(mesh):
    size = mesh.shape["blk"]

    def local(factors, token_mask, store, inv_fisher, source_ids, source_weight):
        if not fits(size, factors, store, inv_fisher):
            return plain(factors, token_mask, store, inv_fisher, source_ids, source_weight)
        scaling = make_scaling(source_ids, source_weight)
        grads = grads_call(factors, token_mask)
        counts = [size // 4, size * 3 // 8, size * 3 // 8]

        def first_stores(after):
            return [load_store(together(store, after)[0], size, k, counts[k]) for k in (0, 1)]

        def last_store(after):
            return load_store(together(store, after)[0], size, 2, counts[2])

        parts, (fisher, stores) = gather_parts(
            grads, size, [lambda after: load_whole(together(inv_fisher, after)[0]), first_stores]
        )
        hidden = fisher_call(parts, fisher, size)
        parts, (last, total) = gather_parts(
            hidden, size, [last_store, lambda chunks: partial_call(chunks, stores[0])]
        )
        total = partial_call(parts[1], stores[1], total)
        return score_call(parts[2], last, total, scaling, factors.shape[0] * size)

    placed = (
        P(("groups", "blk"), None, None, None),
        P(("groups", "blk"), None),
        P(("groups", "blk"), None, None),
        P(None, "blk", None),
        P(("groups", "blk")),
        P(),
    )
    return jax.shard_map(
        local, mesh=mesh, in_specs=placed, out_specs=P("groups", "blk"), check_vma=False
    )
```

```python
import functools
import math

import jax
import jax.numpy as jnp
from jax import lax
from jax.experimental import pallas as pl
from jax.experimental.pallas import tpu as pltpu
from jax.sharding import PartitionSpec as P

LANES = 128
IN_VMEM = pl.BlockSpec(memory_space=pltpu.VMEM)
IN_HBM = pl.BlockSpec(memory_space=pltpu.HBM)
PARAMS = pltpu.CompilerParams(vmem_limit_bytes=16 * 2**20)


def make_grads(factors, token_mask):
    rank_size = factors.shape[3] // 2
    mask_values = token_mask.astype(jnp.float32)[:, None, :, None]
    left_side = factors[..., :rank_size].astype(jnp.float32) * mask_values
    right_side = factors[..., rank_size:].astype(jnp.float32)
    outer_sum = jnp.einsum("qlta,qltb->qlab", left_side, right_side)
    return outer_sum.reshape(outer_sum.shape[0], outer_sum.shape[1], rank_size * rank_size).astype(
        jnp.bfloat16
    )


def make_scaling(source_ids, source_weight):
    matches = (
        source_ids[:, None] == jnp.arange(source_weight.shape[0], dtype=jnp.int32)[None, :]
    ).astype(jnp.float32)
    return jnp.sum(matches * source_weight[None, :], axis=1)


def plain(factors, token_mask, store, inv_fisher, source_ids, source_weight):
    segment = lax.all_gather(make_grads(factors, token_mask), "blk", axis=0, tiled=True)
    products = [
        lax.dot_general(
            segment[:, layer_idx],
            inv_fisher[layer_idx],
            (((1,), (1,)), ((), ())),
            preferred_element_type=jnp.float32,
        )
        for layer_idx in range(inv_fisher.shape[0])
    ]
    hidden_cols = jnp.stack(products, axis=1).astype(jnp.bfloat16)
    hidden = lax.all_gather(hidden_cols, "blk", axis=2, tiled=True)
    raw_scores = lax.dot_general(
        hidden, store, (((1, 2), (1, 2)), ((), ())), preferred_element_type=jnp.float32
    )
    return raw_scores * make_scaling(source_ids, source_weight)[None, :]


def grads_kernel(factors_ref, mask_ref, out_ref, outer_ref, flat_ref):
    queries, layers, _, width = factors_ref.shape
    rank = width // 2
    tiles = rank * rank // LANES
    for layer in range(layers):
        for query in range(queries):
            block = factors_ref[query, layer].astype(jnp.float32)
            left = block[:, :rank].T * mask_ref[query : query + 1]
            outer_ref[...] = jnp.dot(
                left.astype(jnp.bfloat16),
                block[:, rank:].astype(jnp.bfloat16),
                preferred_element_type=jnp.float32,
            )
            flat_ref[layer, pl.ds(query, tiles, queries)] = jnp.concatenate(
                [outer_ref[pl.ds(0, tiles, 2)], outer_ref[pl.ds(1, tiles, 2)]], axis=1
            )
    out_ref[...] = (
        flat_ref[...].astype(jnp.bfloat16).reshape(layers * tiles, queries, LANES)
    )


def grads_call(factors, token_mask):
    queries, layers, _, width = factors.shape
    rank = width // 2
    tiles = rank * rank // LANES
    return pl.pallas_call(
        grads_kernel,
        out_shape=jax.ShapeDtypeStruct((layers * tiles, queries, LANES), jnp.bfloat16),
        in_specs=[IN_VMEM] * 2,
        out_specs=IN_VMEM,
        scratch_shapes=[
            pltpu.VMEM((rank, rank), jnp.float32),
            pltpu.VMEM((layers, tiles * queries, LANES), jnp.float32),
        ],
        compiler_params=PARAMS,
    )(factors, token_mask.astype(jnp.float32))


def load_kernel(size, names, source_ref, out_ref, sem):
    width = out_ref.shape[-1]
    places = owners(size)
    for entry, owner in enumerate(sum([places[name] for name in names], [])):
        columns = pl.ds(pl.multiple_of(owner * width, width), width)
        pltpu.make_async_copy(source_ref.at[:, :, columns], out_ref.at[entry], sem).start()
    pltpu.make_async_copy(out_ref, out_ref, sem).wait()


def load_store(store, size, names, after):
    store, _ = lax.optimization_barrier((store, after))
    rows, layers, feats = store.shape
    entries = sum(entry_count(name, size) for name in names)
    shape = (entries, rows, layers, feats // size)
    return pl.pallas_call(
        functools.partial(load_kernel, size, names),
        out_shape=jax.ShapeDtypeStruct(shape, store.dtype),
        in_specs=[IN_HBM],
        out_specs=IN_VMEM,
        scratch_shapes=[pltpu.SemaphoreType.DMA],
        cost_estimate=pl.CostEstimate(
            flops=0, bytes_accessed=2 * math.prod(shape), transcendentals=0
        ),
        compiler_params=PARAMS,
    )(store)


def copy_kernel(source_ref, out_ref, sem):
    copy = pltpu.make_async_copy(source_ref, out_ref, sem)
    copy.start()
    copy.wait()


def load_whole(source, after):
    source, _ = lax.optimization_barrier((source, after))
    return pl.pallas_call(
        copy_kernel,
        out_shape=jax.ShapeDtypeStruct(source.shape, source.dtype),
        in_specs=[IN_HBM],
        out_specs=IN_VMEM,
        scratch_shapes=[pltpu.SemaphoreType.DMA],
        cost_estimate=pl.CostEstimate(
            flops=0, bytes_accessed=2 * source.size, transcendentals=0
        ),
        compiler_params=PARAMS,
    )(source)


def send(value, even, odd, size):
    pairs = [(i, i ^ (odd if i % 2 else even)) for i in range(size)]
    return lax.ppermute(value, "blk", pairs)


def far_steps(size):
    return [size >> k for k in range(1, size.bit_length()) if size >> k > 4]


def gather_direct(chunk, size, early, middle, late):
    share = chunk[None]
    for step in far_steps(size):
        other = send(share, step, step, size)
        if step == size // 2:
            other, *_ = lax.optimization_barrier((other, *early(share)))
        share = jnp.concatenate([share, other], axis=0)
    got = {"own": share, "core": send(share, 1, 1, size)}
    one, two, three = (send(share, even, odd, size) for even, odd in SQUARE)
    one, got["core"], *_ = lax.optimization_barrier((one, got["core"], *middle(got)))
    got.update(one=one, core_one=send(one, 1, 1, size))
    two, three, *_ = lax.optimization_barrier((two, three, got["core_one"], *late(got)))
    got.update(two=two, core_two=send(two, 1, 1, size))
    got.update(three=three, core_three=send(three, 1, 1, size))
    return got


def gather_square(chunk, size, early, middle, late):
    got = {}
    share = chunk[None]
    for step in far_steps(size):
        other = send(share, step, step, size)
        if step == size // 2:
            other, *_ = lax.optimization_barrier((other, *early(share)))
        share = jnp.concatenate([share, other], axis=0)
    core = send(share, 1, 1, size)
    near = send(share, 4, 4, size)
    got["both"] = jnp.concatenate([share, core], axis=0)
    corner = send(got["both"], 6, 2, size)
    near, *_ = lax.optimization_barrier((near, *middle(got)))
    got["near"] = near
    got["core_near"] = send(near, 1, 1, size)
    corner, *_ = lax.optimization_barrier((corner, got["core_near"], *late(got)))
    got["corner"] = corner
    got["core_corner"] = send(corner, 1, 1, size)
    return got


def owners(size):
    me = lax.axis_index("blk")
    core = me ^ 1
    is_odd = lax.rem(me, 2) == 1
    share = [0]
    for step in far_steps(size):
        share = share + [step ^ entry for entry in share]
    both = share + [1 ^ entry for entry in share]
    places = {
        "own": [me ^ entry for entry in share],
        "core": [core ^ entry for entry in share],
        "both": [me ^ entry for entry in both],
        "near": [me ^ 4 ^ entry for entry in share],
        "core_near": [core ^ 4 ^ entry for entry in share],
    }
    mine, theirs = jnp.where(is_odd, 2, 6), jnp.where(is_odd, 6, 2)
    places["corner"] = [me ^ mine ^ entry for entry in both]
    places["core_corner"] = [core ^ theirs ^ entry for entry in both]
    for name, (even, odd) in zip(("one", "two", "three"), SQUARE):
        mine, theirs = jnp.where(is_odd, odd, even), jnp.where(is_odd, even, odd)
        places[name] = [me ^ mine ^ entry for entry in share]
        places["core_" + name] = [core ^ theirs ^ entry for entry in share]
    return places


def entry_count(name, size):
    return (2 if name in TWICE else 1) << len(far_steps(size))


SQUARE = ((4, 6), (6, 2), (2, 4))
DIRECT = ("own", "core", "one", "two", "three", "core_one", "core_two", "core_three")
TWICE = ("both", "corner", "core_corner")


def fisher_kernel(size, *refs):
    part_refs, (fisher_ref, out_ref, whole_ref) = refs[:-3], refs[-3:]
    layers, rows, feats = fisher_ref.shape
    tiles = feats // LANES
    queries = whole_ref.shape[2]
    places_of = owners(size)
    for ref, name in zip(part_refs, DIRECT):
        for entry, place in enumerate(places_of[name]):
            whole_ref[place] = ref[entry]
    parts = []
    for layer in range(layers):
        grads = jnp.concatenate(
            [
                whole_ref[:, layer * tiles + tile].reshape(size * queries, LANES)
                for tile in range(tiles)
            ],
            axis=1,
        )
        parts.append(
            lax.dot_general(
                fisher_ref[layer],
                grads,
                (((1,), (1,)), ((), ())),
                preferred_element_type=jnp.float32,
            )
        )
    pieces = [
        part[start : start + LANES] for start in range(0, rows, LANES) for part in parts
    ]
    out_ref[...] = jnp.concatenate(pieces, axis=1).astype(jnp.bfloat16)


def fisher_call(got, inv_fisher, size):
    chunk_shape = got["own"].shape[1:]
    return pl.pallas_call(
        functools.partial(fisher_kernel, size),
        out_shape=jax.ShapeDtypeStruct((LANES, LANES), jnp.bfloat16),
        in_specs=[IN_VMEM] * (len(DIRECT) + 1),
        out_specs=IN_VMEM,
        scratch_shapes=[pltpu.VMEM((size,) + chunk_shape, jnp.bfloat16)],
        compiler_params=PARAMS,
    )(*[got[name] for name in DIRECT], inv_fisher)


def products(chunk_refs, store_ref, start, total):
    _, count, layers, width = store_ref.shape
    groups = width // LANES
    span = LANES // groups
    lane = lax.broadcasted_iota(jnp.int32, (LANES, LANES), 1)
    for ref in chunk_refs:
        for entry in range(ref.shape[0]):
            chunk = ref[entry]
            weights = jnp.concatenate(
                [
                    jnp.where(lane // span == group, chunk, jnp.zeros_like(chunk))
                    for group in range(groups)
                ],
                axis=0,
            )
            rows = store_ref[start].reshape(count * layers, width)
            start += 1
            product = jnp.dot(rows, weights, preferred_element_type=jnp.float32)
            total = product if total is None else total + product
    return total


def partial_kernel(starts, *refs):
    number = len(starts)
    total = refs[2 * number][...] if len(refs) == 2 * number + 2 else None
    for chunk_ref, store_ref, start in zip(refs, refs[number:], starts):
        total = products([chunk_ref], store_ref, start, total)
    refs[-1][...] = total


def partial_call(chunks, stores, starts, total=None):
    _, count, layers, width = stores[0].shape
    entries = sum(chunk.shape[0] for chunk in chunks)
    flops = 2 * entries * count * layers * width * LANES
    operands = [*chunks, *stores] + ([] if total is None else [total])
    return pl.pallas_call(
        functools.partial(partial_kernel, tuple(starts)),
        out_shape=jax.ShapeDtypeStruct((count * layers, LANES), jnp.float32),
        in_specs=[IN_VMEM] * len(operands),
        out_specs=IN_VMEM,
        cost_estimate=pl.CostEstimate(flops=0, bytes_accessed=0, transcendentals=0),
        compiler_params=PARAMS,
    )(*operands)


def score_kernel(queries, start, *refs):
    *chunk_refs, store_ref, before_ref, scale_ref, out_ref, total_ref = refs
    _, count, layers, width = store_ref.shape
    span = LANES // (width // LANES)
    total_ref[...] = products(chunk_refs, store_ref, start, before_ref[...])
    lane = lax.broadcasted_iota(jnp.int32, (count, LANES), 1)
    mixed = total_ref[pl.ds(0, count, layers)]
    for layer in range(1, layers):
        rows = total_ref[pl.ds(layer, count, layers)]
        mixed = jnp.where(lane % span // queries == layer, rows, mixed)
    turned = mixed.T
    result = turned[:queries]
    for first in range(queries, LANES, queries):
        result = result + turned[first : first + queries]
    out_ref[...] = result * scale_ref[...]


def score_call(chunks, store, start, total, scaling, queries):
    _, count, layers, _ = store.shape
    return pl.pallas_call(
        functools.partial(score_kernel, queries, start),
        out_shape=jax.ShapeDtypeStruct((queries, count), jnp.float32),
        in_specs=[IN_VMEM] * (len(chunks) + 3),
        out_specs=IN_VMEM,
        scratch_shapes=[pltpu.VMEM(total.shape, jnp.float32)],
        compiler_params=PARAMS,
    )(*chunks, store, total, scaling[None, :])


def fits(size, factors, store, inv_fisher):
    queries, layers, _, width = factors.shape
    _, rows, feats = inv_fisher.shape
    return (
        size >= 16
        and size & (size - 1) == 0
        and width == LANES
        and queries == 2
        and layers == 2
        and rows % LANES == 0
        and (rows // LANES) * layers * queries * size == LANES
        and store.shape[0] % LANES == 0
        and feats == rows * size
    )


def solution(mesh):
    size = mesh.shape["blk"]

    def local(factors, token_mask, store, inv_fisher, source_ids, source_weight):
        if not fits(size, factors, store, inv_fisher):
            return plain(factors, token_mask, store, inv_fisher, source_ids, source_weight)
        scaling = make_scaling(source_ids, source_weight)
        grads = grads_call(factors, token_mask)
        ready = {}

        def keep(name, value):
            ready[name] = value
            return value

        def load(name, parts, after):
            return keep(name, load_store(store, size, parts, after))

        homes = (("both",), ("near", "core_near"), ("corner", "core_corner"))

        def home_of(name):
            return next(k for k, home in enumerate(homes) if name in home)

        def start_of(name):
            home = homes[home_of(name)]
            return sum(entry_count(other, size) for other in home[: home.index(name)])

        got = gather_direct(
            grads,
            size,
            lambda share: [keep("fisher", load_whole(inv_fisher, share))],
            lambda got: [load(0, homes[0], got["core"])],
            lambda got: [load(1, homes[1], got["one"])],
        )
        hidden = fisher_call(got, ready["fisher"], size)

        def add(got, *names):
            total = partial_call(
                [got[name] for name in names],
                [ready[home_of(name)] for name in names],
                [start_of(name) for name in names],
                ready.get("total"),
            )
            return keep("total", total)

        got = gather_square(
            hidden,
            size,
            lambda share: [load(2, homes[2], share)],
            lambda got: [add(got, "both")],
            lambda got: [add(got, "near")],
        )
        add(got, "core_near", "corner")
        return score_call(
            [got["core_corner"]], ready[2], start_of("core_corner"),
            ready["total"], scaling, factors.shape[0] * size,
        )

    placed = (
        P(("groups", "blk"), None, None, None),
        P(("groups", "blk"), None),
        P(("groups", "blk"), None, None),
        P(None, "blk", None),
        P(("groups", "blk")),
        P(),
    )
    return jax.shard_map(
        local, mesh=mesh, in_specs=placed, out_specs=P("groups", "blk"), check_vma=False
    )
```

```python
import functools
import math

import jax
import jax.numpy as jnp
from jax import lax
from jax.experimental import pallas as pl
from jax.experimental.pallas import tpu as pltpu
from jax.sharding import PartitionSpec as P

LANES = 128
IN_VMEM = pl.BlockSpec(memory_space=pltpu.VMEM)
IN_HBM = pl.BlockSpec(memory_space=pltpu.HBM)
PARAMS = pltpu.CompilerParams(vmem_limit_bytes=16 * 2**20)


def make_grads(factors, token_mask):
    rank_size = factors.shape[3] // 2
    mask_values = token_mask.astype(jnp.float32)[:, None, :, None]
    left_side = factors[..., :rank_size].astype(jnp.float32) * mask_values
    right_side = factors[..., rank_size:].astype(jnp.float32)
    outer_sum = jnp.einsum("qlta,qltb->qlab", left_side, right_side)
    return outer_sum.reshape(outer_sum.shape[0], outer_sum.shape[1], rank_size * rank_size).astype(
        jnp.bfloat16
    )


def make_scaling(source_ids, source_weight):
    matches = (
        source_ids[:, None] == jnp.arange(source_weight.shape[0], dtype=jnp.int32)[None, :]
    ).astype(jnp.float32)
    return jnp.sum(matches * source_weight[None, :], axis=1)


def plain(factors, token_mask, store, inv_fisher, source_ids, source_weight):
    segment = lax.all_gather(make_grads(factors, token_mask), "blk", axis=0, tiled=True)
    products = [
        lax.dot_general(
            segment[:, layer_idx],
            inv_fisher[layer_idx],
            (((1,), (1,)), ((), ())),
            preferred_element_type=jnp.float32,
        )
        for layer_idx in range(inv_fisher.shape[0])
    ]
    hidden_cols = jnp.stack(products, axis=1).astype(jnp.bfloat16)
    hidden = lax.all_gather(hidden_cols, "blk", axis=2, tiled=True)
    raw_scores = lax.dot_general(
        hidden, store, (((1, 2), (1, 2)), ((), ())), preferred_element_type=jnp.float32
    )
    return raw_scores * make_scaling(source_ids, source_weight)[None, :]


def grads_kernel(factors_ref, mask_ref, out_ref, outer_ref, flat_ref):
    queries, layers, _, width = factors_ref.shape
    rank = width // 2
    tiles = rank * rank // LANES
    for layer in range(layers):
        for query in range(queries):
            block = factors_ref[query, layer].astype(jnp.float32)
            left = block[:, :rank].T * mask_ref[query : query + 1].astype(jnp.float32)
            outer_ref[...] = jnp.dot(
                left.astype(jnp.bfloat16),
                block[:, rank:].astype(jnp.bfloat16),
                preferred_element_type=jnp.float32,
            )
            flat_ref[layer, pl.ds(query, tiles, queries)] = jnp.concatenate(
                [outer_ref[pl.ds(0, tiles, 2)], outer_ref[pl.ds(1, tiles, 2)]], axis=1
            )
    out_ref[...] = (
        flat_ref[...].astype(jnp.bfloat16).reshape(layers * tiles, queries, LANES)
    )


def grads_call(factors, token_mask):
    queries, layers, _, width = factors.shape
    rank = width // 2
    tiles = rank * rank // LANES
    return pl.pallas_call(
        grads_kernel,
        out_shape=jax.ShapeDtypeStruct((layers * tiles, queries, LANES), jnp.bfloat16),
        grid=(1,),
        in_specs=[
            pl.BlockSpec(factors.shape, lambda i: (0, 0, 0, 0)),
            pl.BlockSpec(token_mask.shape, lambda i: (0, 0)),
        ],
        out_specs=pl.BlockSpec((layers * tiles, queries, LANES), lambda i: (0, 0, 0)),
        scratch_shapes=[
            pltpu.VMEM((rank, rank), jnp.float32),
            pltpu.VMEM((layers, tiles * queries, LANES), jnp.float32),
        ],
        compiler_params=PARAMS,
    )(factors, token_mask)


def load_kernel(size, names, source_ref, out_ref, sem):
    width = out_ref.shape[-1]
    places = owners(size)
    for entry, owner in enumerate(sum([places[name] for name in names], [])):
        columns = pl.ds(pl.multiple_of(owner * width, width), width)
        pltpu.make_async_copy(source_ref.at[:, :, columns], out_ref.at[entry], sem).start()
    pltpu.make_async_copy(out_ref, out_ref, sem).wait()


def load_store(store, size, names, after):
    store, _ = lax.optimization_barrier((store, after))
    rows, layers, feats = store.shape
    entries = len(names) * entry_count(size)
    shape = (entries, rows, layers, feats // size)
    return pl.pallas_call(
        functools.partial(load_kernel, size, names),
        out_shape=jax.ShapeDtypeStruct(shape, store.dtype),
        in_specs=[IN_HBM],
        out_specs=IN_VMEM,
        scratch_shapes=[pltpu.SemaphoreType.DMA],
        cost_estimate=pl.CostEstimate(
            flops=0, bytes_accessed=2 * math.prod(shape), transcendentals=0
        ),
        compiler_params=PARAMS,
    )(store)


def copy_kernel(source_ref, out_ref, sem):
    copy = pltpu.make_async_copy(source_ref, out_ref, sem)
    copy.start()
    copy.wait()


def load_whole(source, after):
    source, _ = lax.optimization_barrier((source, after))
    return pl.pallas_call(
        copy_kernel,
        out_shape=jax.ShapeDtypeStruct(source.shape, source.dtype),
        in_specs=[IN_HBM],
        out_specs=IN_VMEM,
        scratch_shapes=[pltpu.SemaphoreType.DMA],
        cost_estimate=pl.CostEstimate(
            flops=0, bytes_accessed=2 * source.size, transcendentals=0
        ),
        compiler_params=PARAMS,
    )(source)


def send(value, even, odd, size):
    pairs = [(i, i ^ (odd if i % 2 else even)) for i in range(size)]
    return lax.ppermute(value, "blk", pairs)


def far_steps(size):
    return [size >> k for k in range(1, size.bit_length()) if size >> k > 4]


def gather(chunk, size, early, middle, late):
    share = chunk[None]
    for step in far_steps(size):
        other = send(share, step ^ 1, step ^ 1, size)
        if step == size // 2:
            other, *_ = lax.optimization_barrier((other, *early(share)))
        share = jnp.concatenate([share, other], axis=0)
    got = {"own": share, "core": send(share, 1, 1, size)}
    one, two, three = (send(share, even, odd, size) for even, odd in SQUARE)
    one, got["core"], *_ = lax.optimization_barrier((one, got["core"], *middle(got)))
    got.update(one=one, core_one=send(one, 1, 1, size))
    two, three, *_ = lax.optimization_barrier((two, three, got["core_one"], *late(got)))
    got.update(two=two, core_two=send(two, 1, 1, size))
    got.update(three=three, core_three=send(three, 1, 1, size))
    return got


def owners(size):
    me = lax.axis_index("blk")
    core = me ^ 1
    is_odd = lax.rem(me, 2) == 1
    share = [0]
    for step in far_steps(size):
        share = share + [step ^ 1 ^ entry for entry in share]
    places = {"own": [me ^ entry for entry in share], "core": [core ^ entry for entry in share]}
    for name, (even, odd) in zip(("one", "two", "three"), SQUARE):
        mine, theirs = jnp.where(is_odd, even, odd), jnp.where(is_odd, odd, even)
        places[name] = [me ^ mine ^ entry for entry in share]
        places["core_" + name] = [core ^ theirs ^ entry for entry in share]
    return places


def entry_count(size):
    return 1 << len(far_steps(size))


SQUARE = ((7, 7), (5, 5), (3, 3))
NAMES = ("own", "core", "one", "two", "three", "core_one", "core_two", "core_three")


def fisher_kernel(size, *refs):
    part_refs, (fisher_ref, out_ref, whole_ref) = refs[:-3], refs[-3:]
    layers, rows, feats = fisher_ref.shape
    tiles = feats // LANES
    queries = whole_ref.shape[2]
    places_of = owners(size)
    for ref, name in zip(part_refs, NAMES):
        for entry, place in enumerate(places_of[name]):
            whole_ref[place] = ref[entry]
    parts = []
    for layer in range(layers):
        grads = jnp.concatenate(
            [
                whole_ref[:, layer * tiles + tile].reshape(size * queries, LANES)
                for tile in range(tiles)
            ],
            axis=1,
        )
        parts.append(
            lax.dot_general(
                fisher_ref[layer],
                grads,
                (((1,), (1,)), ((), ())),
                preferred_element_type=jnp.float32,
            )
        )
    pieces = [
        part[start : start + LANES] for start in range(0, rows, LANES) for part in parts
    ]
    out_ref[...] = jnp.concatenate(pieces, axis=1).astype(jnp.bfloat16)


def fisher_call(got, inv_fisher, size):
    chunk_shape = got["own"].shape[1:]
    return pl.pallas_call(
        functools.partial(fisher_kernel, size),
        out_shape=jax.ShapeDtypeStruct((LANES, LANES), jnp.bfloat16),
        in_specs=[IN_VMEM] * (len(NAMES) + 1),
        out_specs=IN_VMEM,
        scratch_shapes=[pltpu.VMEM((size,) + chunk_shape, jnp.bfloat16)],
        compiler_params=PARAMS,
    )(*[got[name] for name in NAMES], inv_fisher)


def products(chunk_refs, store_ref, start, total):
    _, count, layers, width = store_ref.shape
    groups = width // LANES
    span = LANES // groups
    lane = lax.broadcasted_iota(jnp.int32, (LANES, LANES), 1)
    for ref in chunk_refs:
        for entry in range(ref.shape[0]):
            chunk = ref[entry]
            weights = jnp.concatenate(
                [
                    jnp.where(lane // span == group, chunk, jnp.zeros_like(chunk))
                    for group in range(groups)
                ],
                axis=0,
            )
            rows = store_ref[start].reshape(count * layers, width)
            start += 1
            product = jnp.dot(rows, weights, preferred_element_type=jnp.float32)
            total = product if total is None else total + product
    return total


def partial_kernel(starts, *refs):
    number = len(starts)
    total = refs[2 * number][...] if len(refs) == 2 * number + 2 else None
    for chunk_ref, store_ref, start in zip(refs, refs[number:], starts):
        total = products([chunk_ref], store_ref, start, total)
    refs[-1][...] = total


def partial_call(chunks, stores, starts, total=None):
    _, count, layers, width = stores[0].shape
    entries = sum(chunk.shape[0] for chunk in chunks)
    flops = 2 * entries * count * layers * width * LANES
    operands = [*chunks, *stores] + ([] if total is None else [total])
    return pl.pallas_call(
        functools.partial(partial_kernel, tuple(starts)),
        out_shape=jax.ShapeDtypeStruct((count * layers, LANES), jnp.float32),
        in_specs=[IN_VMEM] * len(operands),
        out_specs=IN_VMEM,
        cost_estimate=pl.CostEstimate(flops=0, bytes_accessed=0, transcendentals=0),
        compiler_params=PARAMS,
    )(*operands)


def score_kernel(queries, start, *refs):
    *chunk_refs, store_ref, before_ref, scale_ref, out_ref, total_ref = refs
    _, count, layers, width = store_ref.shape
    span = LANES // (width // LANES)
    total_ref[...] = products(chunk_refs, store_ref, start, before_ref[...])
    lane = lax.broadcasted_iota(jnp.int32, (count, LANES), 1)
    mixed = total_ref[pl.ds(0, count, layers)]
    for layer in range(1, layers):
        rows = total_ref[pl.ds(layer, count, layers)]
        mixed = jnp.where(lane % span // queries == layer, rows, mixed)
    turned = mixed.T
    result = turned[:queries]
    for first in range(queries, LANES, queries):
        result = result + turned[first : first + queries]
    out_ref[...] = result * scale_ref[...]


def score_call(chunks, store, start, total, scaling, queries):
    _, count, layers, _ = store.shape
    return pl.pallas_call(
        functools.partial(score_kernel, queries, start),
        out_shape=jax.ShapeDtypeStruct((queries, count), jnp.float32),
        in_specs=[IN_VMEM] * (len(chunks) + 3),
        out_specs=IN_VMEM,
        scratch_shapes=[pltpu.VMEM(total.shape, jnp.float32)],
        compiler_params=PARAMS,
    )(*chunks, store, total, scaling[None, :])


def fits(size, factors, store, inv_fisher):
    queries, layers, _, width = factors.shape
    _, rows, feats = inv_fisher.shape
    return (
        size >= 16
        and size & (size - 1) == 0
        and width == LANES
        and queries == 2
        and layers == 2
        and rows % LANES == 0
        and (rows // LANES) * layers * queries * size == LANES
        and store.shape[0] % LANES == 0
        and feats == rows * size
    )


def solution(mesh):
    size = mesh.shape["blk"]

    def local(factors, token_mask, store, inv_fisher, source_ids, source_weight):
        if not fits(size, factors, store, inv_fisher):
            return plain(factors, token_mask, store, inv_fisher, source_ids, source_weight)
        scaling = make_scaling(source_ids, source_weight)
        grads = grads_call(factors, token_mask)
        ready = {}

        def keep(name, value):
            ready[name] = value
            return value

        def load(name, parts, after):
            return keep(name, load_store(store, size, parts, after))

        homes = (("own", "core"), ("one", "core_one"), ("two", "three", "core_two", "core_three"))

        def home_of(name):
            return next(k for k, home in enumerate(homes) if name in home)

        def start_of(name):
            return homes[home_of(name)].index(name) * entry_count(size)

        got = gather(
            grads,
            size,
            lambda share: [keep("fisher", load_whole(inv_fisher, share))],
            lambda got: [load(0, homes[0], got["core"])],
            lambda got: [load(1, homes[1], got["one"])],
        )
        hidden = fisher_call(got, ready["fisher"], size)

        def add(got, *names):
            total = partial_call(
                [got[name] for name in names],
                [ready[home_of(name)] for name in names],
                [start_of(name) for name in names],
                ready.get("total"),
            )
            return keep("total", total)

        got = gather(
            hidden,
            size,
            lambda share: [load(2, homes[2], share)],
            lambda got: [add(got, "own", "core")],
            lambda got: [add(got, "one")],
        )
        add(got, "core_one", "two", "three")
        return score_call(
            [got["core_two"], got["core_three"]], ready[2], start_of("core_two"),
            ready["total"], scaling, factors.shape[0] * size,
        )

    placed = (
        P(("groups", "blk"), None, None, None),
        P(("groups", "blk"), None),
        P(("groups", "blk"), None, None),
        P(None, "blk", None),
        P(("groups", "blk")),
        P(),
    )
    return jax.shard_map(
        local, mesh=mesh, in_specs=placed, out_specs=P("groups", "blk"), check_vma=False
    )
```

```python
import functools
import math

import jax
import jax.numpy as jnp
from jax import lax
from jax.experimental import pallas as pl
from jax.experimental.pallas import tpu as pltpu
from jax.sharding import PartitionSpec as P

LANES = 128
IN_VMEM = pl.BlockSpec(memory_space=pltpu.VMEM)
IN_HBM = pl.BlockSpec(memory_space=pltpu.HBM)
PARAMS = pltpu.CompilerParams(vmem_limit_bytes=16 * 2**20)


def make_grads(factors, token_mask):
    rank_size = factors.shape[3] // 2
    mask_values = token_mask.astype(jnp.float32)[:, None, :, None]
    left_side = factors[..., :rank_size].astype(jnp.float32) * mask_values
    right_side = factors[..., rank_size:].astype(jnp.float32)
    outer_sum = jnp.einsum("qlta,qltb->qlab", left_side, right_side)
    return outer_sum.reshape(outer_sum.shape[0], outer_sum.shape[1], rank_size * rank_size).astype(
        jnp.bfloat16
    )


def make_scaling(source_ids, source_weight):
    matches = (
        source_ids[:, None] == jnp.arange(source_weight.shape[0], dtype=jnp.int32)[None, :]
    ).astype(jnp.float32)
    return jnp.sum(matches * source_weight[None, :], axis=1)


def plain(factors, token_mask, store, inv_fisher, source_ids, source_weight):
    segment = lax.all_gather(make_grads(factors, token_mask), "blk", axis=0, tiled=True)
    products = [
        lax.dot_general(
            segment[:, layer_idx],
            inv_fisher[layer_idx],
            (((1,), (1,)), ((), ())),
            preferred_element_type=jnp.float32,
        )
        for layer_idx in range(inv_fisher.shape[0])
    ]
    hidden_cols = jnp.stack(products, axis=1).astype(jnp.bfloat16)
    hidden = lax.all_gather(hidden_cols, "blk", axis=2, tiled=True)
    raw_scores = lax.dot_general(
        hidden, store, (((1, 2), (1, 2)), ((), ())), preferred_element_type=jnp.float32
    )
    return raw_scores * make_scaling(source_ids, source_weight)[None, :]


def grads_kernel(factors_ref, mask_ref, out_ref, outer_ref, flat_ref):
    queries, layers, _, width = factors_ref.shape
    rank = width // 2
    tiles = rank * rank // LANES
    for layer in range(layers):
        for query in range(queries):
            block = factors_ref[query, layer].astype(jnp.float32)
            left = block[:, :rank].T * mask_ref[query : query + 1].astype(jnp.float32)
            outer_ref[...] = jnp.dot(
                left.astype(jnp.bfloat16),
                block[:, rank:].astype(jnp.bfloat16),
                preferred_element_type=jnp.float32,
            )
            flat_ref[layer, pl.ds(query, tiles, queries)] = jnp.concatenate(
                [outer_ref[pl.ds(0, tiles, 2)], outer_ref[pl.ds(1, tiles, 2)]], axis=1
            )
    out_ref[...] = (
        flat_ref[...].astype(jnp.bfloat16).reshape(layers * tiles, queries, LANES)
    )


def grads_call(factors, token_mask):
    queries, layers, _, width = factors.shape
    rank = width // 2
    tiles = rank * rank // LANES
    return pl.pallas_call(
        grads_kernel,
        out_shape=jax.ShapeDtypeStruct((layers * tiles, queries, LANES), jnp.bfloat16),
        grid=(1,),
        in_specs=[
            pl.BlockSpec(factors.shape, lambda i: (0, 0, 0, 0)),
            pl.BlockSpec(token_mask.shape, lambda i: (0, 0)),
        ],
        out_specs=pl.BlockSpec((layers * tiles, queries, LANES), lambda i: (0, 0, 0)),
        scratch_shapes=[
            pltpu.VMEM((rank, rank), jnp.float32),
            pltpu.VMEM((layers, tiles * queries, LANES), jnp.float32),
        ],
        cost_estimate=pl.CostEstimate(flops=10**10, bytes_accessed=0, transcendentals=0),
        compiler_params=PARAMS,
    )(factors, token_mask)


def load_kernel(size, names, source_ref, out_ref, sem):
    width = out_ref.shape[-1]
    places = owners(size, SECOND)
    for entry, owner in enumerate(sum([places[name] for name in names], [])):
        columns = pl.ds(pl.multiple_of(owner * width, width), width)
        pltpu.make_async_copy(source_ref.at[:, :, columns], out_ref.at[entry], sem).start()
    pltpu.make_async_copy(out_ref, out_ref, sem).wait()


def load_store(store, size, names, after):
    store, _ = lax.optimization_barrier((store, after))
    rows, layers, feats = store.shape
    entries = len(names) * entry_count(size)
    shape = (entries, rows, layers, feats // size)
    return pl.pallas_call(
        functools.partial(load_kernel, size, names),
        out_shape=jax.ShapeDtypeStruct(shape, store.dtype),
        in_specs=[IN_HBM],
        out_specs=IN_VMEM,
        scratch_shapes=[pltpu.SemaphoreType.DMA],
        cost_estimate=pl.CostEstimate(
            flops=0, bytes_accessed=2 * math.prod(shape), transcendentals=0
        ),
        compiler_params=PARAMS,
    )(store)


def copy_kernel(source_ref, out_ref, sem):
    copy = pltpu.make_async_copy(source_ref, out_ref, sem)
    copy.start()
    copy.wait()


def load_whole(source, after):
    source, _ = lax.optimization_barrier((source, after))
    return pl.pallas_call(
        copy_kernel,
        out_shape=jax.ShapeDtypeStruct(source.shape, source.dtype),
        in_specs=[IN_HBM],
        out_specs=IN_VMEM,
        scratch_shapes=[pltpu.SemaphoreType.DMA],
        cost_estimate=pl.CostEstimate(
            flops=0, bytes_accessed=2 * source.size, transcendentals=0
        ),
        compiler_params=PARAMS,
    )(source)


def send(value, even, odd, size):
    pairs = [(i, i ^ (odd if i % 2 else even)) for i in range(size)]
    return lax.ppermute(value, "blk", pairs)


def far_steps(size):
    return [size >> k for k in range(1, size.bit_length()) if size >> k > 4]


def gather(chunk, size, plan, early, middle, late):
    share = chunk[None]
    for step in far_steps(size):
        other = send(share, step ^ plan[0], step ^ plan[0], size)
        if step == size // 2:
            other, *_ = lax.optimization_barrier((other, *early(share)))
        share = jnp.concatenate([share, other], axis=0)
    got = {"own": share, "core": send(share, 1, 1, size)}
    one, two, three = (send(share, even, odd, size) for even, odd in plan[1])
    one, got["core"], *_ = lax.optimization_barrier((one, got["core"], *middle(got)))
    got.update(one=one, core_one=send(one, 1, 1, size))
    two, three, *_ = lax.optimization_barrier((two, three, got["core_one"], *late(got)))
    got.update(two=two, core_two=send(two, 1, 1, size))
    got.update(three=three, core_three=send(three, 1, 1, size))
    return got


def owners(size, plan):
    me = lax.axis_index("blk")
    core = me ^ 1
    is_odd = lax.rem(me, 2) == 1
    share = [0]
    for step in far_steps(size):
        share = share + [step ^ plan[0] ^ entry for entry in share]
    places = {"own": [me ^ entry for entry in share], "core": [core ^ entry for entry in share]}
    for name, (even, odd) in zip(("one", "two", "three"), plan[1]):
        if even % 2:
            even, odd = odd, even
        mine, theirs = jnp.where(is_odd, odd, even), jnp.where(is_odd, even, odd)
        places[name] = [me ^ mine ^ entry for entry in share]
        places["core_" + name] = [core ^ theirs ^ entry for entry in share]
    return places


def entry_count(size):
    return 1 << len(far_steps(size))


FIRST = (1, ((7, 7), (5, 5), (3, 3)))
SECOND = (1, ((7, 7), (5, 5), (3, 3)))
NAMES = ("own", "core", "one", "two", "three", "core_one", "core_two", "core_three")


def fisher_kernel(size, *refs):
    part_refs, (fisher_ref, out_ref, whole_ref) = refs[:-3], refs[-3:]
    layers, rows, feats = fisher_ref.shape
    tiles = feats // LANES
    queries = whole_ref.shape[2]
    places_of = owners(size, FIRST)
    for ref, name in zip(part_refs, NAMES):
        for entry, place in enumerate(places_of[name]):
            whole_ref[place] = ref[entry]
    parts = []
    for layer in range(layers):
        grads = jnp.concatenate(
            [
                whole_ref[:, layer * tiles + tile].reshape(size * queries, LANES)
                for tile in range(tiles)
            ],
            axis=1,
        )
        parts.append(
            lax.dot_general(
                fisher_ref[layer],
                grads,
                (((1,), (1,)), ((), ())),
                preferred_element_type=jnp.float32,
            )
        )
    pieces = [
        part[start : start + LANES] for start in range(0, rows, LANES) for part in parts
    ]
    out_ref[...] = jnp.concatenate(pieces, axis=1).astype(jnp.bfloat16)


def fisher_call(got, inv_fisher, size):
    chunk_shape = got["own"].shape[1:]
    return pl.pallas_call(
        functools.partial(fisher_kernel, size),
        out_shape=jax.ShapeDtypeStruct((LANES, LANES), jnp.bfloat16),
        in_specs=[IN_VMEM] * (len(NAMES) + 1),
        out_specs=IN_VMEM,
        scratch_shapes=[pltpu.VMEM((size,) + chunk_shape, jnp.bfloat16)],
        compiler_params=PARAMS,
    )(*[got[name] for name in NAMES], inv_fisher)


def products(chunk_refs, store_ref, start, total):
    _, count, layers, width = store_ref.shape
    groups = width // LANES
    span = LANES // groups
    lane = lax.broadcasted_iota(jnp.int32, (LANES, LANES), 1)
    for ref in chunk_refs:
        for entry in range(ref.shape[0]):
            chunk = ref[entry]
            weights = jnp.concatenate(
                [
                    jnp.where(lane // span == group, chunk, jnp.zeros_like(chunk))
                    for group in range(groups)
                ],
                axis=0,
            )
            rows = store_ref[start].reshape(count * layers, width)
            start += 1
            product = jnp.dot(rows, weights, preferred_element_type=jnp.float32)
            total = product if total is None else total + product
    return total


def partial_kernel(starts, *refs):
    number = len(starts)
    total = refs[2 * number][...] if len(refs) == 2 * number + 2 else None
    for chunk_ref, store_ref, start in zip(refs, refs[number:], starts):
        total = products([chunk_ref], store_ref, start, total)
    refs[-1][...] = total


def partial_call(chunks, stores, starts, total=None):
    _, count, layers, width = stores[0].shape
    entries = sum(chunk.shape[0] for chunk in chunks)
    flops = 2 * entries * count * layers * width * LANES
    operands = [*chunks, *stores] + ([] if total is None else [total])
    return pl.pallas_call(
        functools.partial(partial_kernel, tuple(starts)),
        out_shape=jax.ShapeDtypeStruct((count * layers, LANES), jnp.float32),
        in_specs=[IN_VMEM] * len(operands),
        out_specs=IN_VMEM,
        cost_estimate=pl.CostEstimate(flops=0, bytes_accessed=0, transcendentals=0),
        compiler_params=PARAMS,
    )(*operands)


def score_kernel(queries, start, *refs):
    *chunk_refs, store_ref, before_ref, scale_ref, out_ref, total_ref = refs
    _, count, layers, width = store_ref.shape
    span = LANES // (width // LANES)
    total_ref[...] = products(chunk_refs, store_ref, start, before_ref[...])
    lane = lax.broadcasted_iota(jnp.int32, (count, LANES), 1)
    mixed = total_ref[pl.ds(0, count, layers)]
    for layer in range(1, layers):
        rows = total_ref[pl.ds(layer, count, layers)]
        mixed = jnp.where(lane % span // queries == layer, rows, mixed)
    turned = mixed.T
    result = turned[:queries]
    for first in range(queries, LANES, queries):
        result = result + turned[first : first + queries]
    out_ref[...] = result * scale_ref[...]


def score_call(chunks, store, start, total, scaling, queries):
    _, count, layers, _ = store.shape
    return pl.pallas_call(
        functools.partial(score_kernel, queries, start),
        out_shape=jax.ShapeDtypeStruct((queries, count), jnp.float32),
        in_specs=[IN_VMEM] * (len(chunks) + 3),
        out_specs=IN_VMEM,
        scratch_shapes=[pltpu.VMEM(total.shape, jnp.float32)],
        compiler_params=PARAMS,
    )(*chunks, store, total, scaling[None, :])


def fits(size, factors, store, inv_fisher):
    queries, layers, _, width = factors.shape
    _, rows, feats = inv_fisher.shape
    return (
        size >= 16
        and size & (size - 1) == 0
        and width == LANES
        and queries == 2
        and layers == 2
        and rows % LANES == 0
        and (rows // LANES) * layers * queries * size == LANES
        and store.shape[0] % LANES == 0
        and feats == rows * size
    )


def solution(mesh):
    size = mesh.shape["blk"]

    def local(factors, token_mask, store, inv_fisher, source_ids, source_weight):
        if not fits(size, factors, store, inv_fisher):
            return plain(factors, token_mask, store, inv_fisher, source_ids, source_weight)
        scaling = make_scaling(source_ids, source_weight)
        grads = grads_call(factors, token_mask)
        ready = {}

        def keep(name, value):
            ready[name] = value
            return value

        def load(name, parts, after):
            return keep(name, load_store(store, size, parts, after))

        homes = (
            ("own", "core"),
            ("one", "core_one"),
            ("two", "three"),
            ("core_two", "core_three"),
        )

        def home_of(name):
            return next(k for k, home in enumerate(homes) if name in home)

        def start_of(name):
            return homes[home_of(name)].index(name) * entry_count(size)

        got = gather(
            grads,
            size,
            FIRST,
            lambda share: [keep("fisher", load_whole(inv_fisher, share))],
            lambda got: [load(0, homes[0], got["core"])],
            lambda got: [load(1, homes[1], got["one"])],
        )
        hidden = fisher_call(got, ready["fisher"], size)

        def add(got, *names):
            total = partial_call(
                [got[name] for name in names],
                [ready[home_of(name)] for name in names],
                [start_of(name) for name in names],
                ready.get("total"),
            )
            return keep("total", total)

        got = gather(
            hidden,
            size,
            SECOND,
            lambda share: [load(2, homes[2], share)],
            lambda got: [add(got, "own", "core"), load(3, homes[3], got["core"])],
            lambda got: [add(got, "one")],
        )
        add(got, "core_one", "two", "three")
        return score_call(
            [got["core_two"], got["core_three"]], ready[3], start_of("core_two"),
            ready["total"], scaling, factors.shape[0] * size,
        )

    placed = (
        P(("groups", "blk"), None, None, None),
        P(("groups", "blk"), None),
        P(("groups", "blk"), None, None),
        P(None, "blk", None),
        P(("groups", "blk")),
        P(),
    )
    return jax.shard_map(
        local, mesh=mesh, in_specs=placed, out_specs=P("groups", "blk"), check_vma=False
    )
```

```python
import functools
import math

import jax
import jax.numpy as jnp
from jax import lax
from jax.experimental import pallas as pl
from jax.experimental.pallas import tpu as pltpu
from jax.sharding import PartitionSpec as P

LANES = 128
IN_VMEM = pl.BlockSpec(memory_space=pltpu.VMEM)
IN_HBM = pl.BlockSpec(memory_space=pltpu.HBM)
PARAMS = pltpu.CompilerParams(vmem_limit_bytes=16 * 2**20)


def make_grads(factors, token_mask):
    rank_size = factors.shape[3] // 2
    mask_values = token_mask.astype(jnp.float32)[:, None, :, None]
    left_side = factors[..., :rank_size].astype(jnp.float32) * mask_values
    right_side = factors[..., rank_size:].astype(jnp.float32)
    outer_sum = jnp.einsum("qlta,qltb->qlab", left_side, right_side)
    return outer_sum.reshape(outer_sum.shape[0], outer_sum.shape[1], rank_size * rank_size).astype(
        jnp.bfloat16
    )


def make_scaling(source_ids, source_weight):
    matches = (
        source_ids[:, None] == jnp.arange(source_weight.shape[0], dtype=jnp.int32)[None, :]
    ).astype(jnp.float32)
    return jnp.sum(matches * source_weight[None, :], axis=1)


def plain(factors, token_mask, store, inv_fisher, source_ids, source_weight):
    segment = lax.all_gather(make_grads(factors, token_mask), "blk", axis=0, tiled=True)
    products = [
        lax.dot_general(
            segment[:, layer_idx],
            inv_fisher[layer_idx],
            (((1,), (1,)), ((), ())),
            preferred_element_type=jnp.float32,
        )
        for layer_idx in range(inv_fisher.shape[0])
    ]
    hidden_cols = jnp.stack(products, axis=1).astype(jnp.bfloat16)
    hidden = lax.all_gather(hidden_cols, "blk", axis=2, tiled=True)
    raw_scores = lax.dot_general(
        hidden, store, (((1, 2), (1, 2)), ((), ())), preferred_element_type=jnp.float32
    )
    return raw_scores * make_scaling(source_ids, source_weight)[None, :]


def grads_kernel(factors_ref, mask_ref, out_ref, outer_ref, flat_ref):
    queries, layers, _, width = factors_ref.shape
    rank = width // 2
    tiles = rank * rank // LANES
    for layer in range(layers):
        for query in range(queries):
            block = factors_ref[query, layer].astype(jnp.float32)
            left = block[:, :rank].T * mask_ref[query : query + 1].astype(jnp.float32)
            outer_ref[...] = jnp.dot(
                left.astype(jnp.bfloat16),
                block[:, rank:].astype(jnp.bfloat16),
                preferred_element_type=jnp.float32,
            )
            flat_ref[layer, pl.ds(query, tiles, queries)] = jnp.concatenate(
                [outer_ref[pl.ds(0, tiles, 2)], outer_ref[pl.ds(1, tiles, 2)]], axis=1
            )
    out_ref[...] = (
        flat_ref[...].astype(jnp.bfloat16).reshape(layers * tiles, queries, LANES)
    )


def grads_call(factors, token_mask):
    queries, layers, _, width = factors.shape
    rank = width // 2
    tiles = rank * rank // LANES
    return pl.pallas_call(
        grads_kernel,
        out_shape=jax.ShapeDtypeStruct((layers * tiles, queries, LANES), jnp.bfloat16),
        grid=(1,),
        in_specs=[
            pl.BlockSpec(factors.shape, lambda i: (0, 0, 0, 0)),
            pl.BlockSpec(token_mask.shape, lambda i: (0, 0)),
        ],
        out_specs=pl.BlockSpec((layers * tiles, queries, LANES), lambda i: (0, 0, 0)),
        scratch_shapes=[
            pltpu.VMEM((rank, rank), jnp.float32),
            pltpu.VMEM((layers, tiles * queries, LANES), jnp.float32),
        ],
        cost_estimate=pl.CostEstimate(flops=10**10, bytes_accessed=0, transcendentals=0),
        compiler_params=PARAMS,
    )(factors, token_mask)


def load_kernel(size, names, source_ref, out_ref, sem):
    width = out_ref.shape[-1]
    places = owners(size, SECOND)
    for entry, owner in enumerate(sum([places[name] for name in names], [])):
        columns = pl.ds(pl.multiple_of(owner * width, width), width)
        pltpu.make_async_copy(source_ref.at[:, :, columns], out_ref.at[entry], sem).start()
    pltpu.make_async_copy(out_ref, out_ref, sem).wait()


def load_store(store, size, names, after):
    store, _ = lax.optimization_barrier((store, after))
    rows, layers, feats = store.shape
    entries = len(names) * entry_count(size)
    shape = (entries, rows, layers, feats // size)
    return pl.pallas_call(
        functools.partial(load_kernel, size, names),
        out_shape=jax.ShapeDtypeStruct(shape, store.dtype),
        in_specs=[IN_HBM],
        out_specs=IN_VMEM,
        scratch_shapes=[pltpu.SemaphoreType.DMA],
        cost_estimate=pl.CostEstimate(
            flops=0, bytes_accessed=2 * math.prod(shape), transcendentals=0
        ),
        compiler_params=PARAMS,
    )(store)


def copy_kernel(source_ref, out_ref, sem):
    copy = pltpu.make_async_copy(source_ref, out_ref, sem)
    copy.start()
    copy.wait()


def load_whole(source, after):
    source, _ = lax.optimization_barrier((source, after))
    return pl.pallas_call(
        copy_kernel,
        out_shape=jax.ShapeDtypeStruct(source.shape, source.dtype),
        in_specs=[IN_HBM],
        out_specs=IN_VMEM,
        scratch_shapes=[pltpu.SemaphoreType.DMA],
        cost_estimate=pl.CostEstimate(
            flops=0, bytes_accessed=2 * source.size, transcendentals=0
        ),
        compiler_params=PARAMS,
    )(source)


def send(value, even, odd, size):
    pairs = [(i, i ^ (odd if i % 2 else even)) for i in range(size)]
    return lax.ppermute(value, "blk", pairs)


def far_steps(size):
    return [size >> k for k in range(1, size.bit_length()) if size >> k > 4]


def gather(chunk, size, plan, early, middle, late):
    flip, square, late_core = plan
    share = chunk[None]
    for step in far_steps(size):
        other = send(share, step ^ flip, step ^ flip, size)
        if step == size // 2:
            other, *_ = lax.optimization_barrier((other, *early(share)))
        share = jnp.concatenate([share, other], axis=0)
    one, two, three = (send(share, even, odd, size) for even, odd in square)
    got = {"own": share}
    if late_core:
        one, *_ = lax.optimization_barrier((one, *middle(got)))
        held, _ = lax.optimization_barrier((share, one))
        got["core"] = send(held, 1, 1, size)
    else:
        got["core"] = send(share, 1, 1, size)
        one, got["core"], *_ = lax.optimization_barrier((one, got["core"], *middle(got)))
    got.update(one=one, core_one=send(one, 1, 1, size))
    two, three, *_ = lax.optimization_barrier(
        (two, three, got["core"], got["core_one"], *late(got))
    )
    got.update(two=two, core_two=send(two, 1, 1, size))
    got.update(three=three, core_three=send(three, 1, 1, size))
    return got


def owners(size, plan):
    me = lax.axis_index("blk")
    core = me ^ 1
    is_odd = lax.rem(me, 2) == 1
    share = [0]
    for step in far_steps(size):
        share = share + [step ^ plan[0] ^ entry for entry in share]
    places = {"own": [me ^ entry for entry in share], "core": [core ^ entry for entry in share]}
    for name, (even, odd) in zip(("one", "two", "three"), plan[1]):
        if even % 2:
            even, odd = odd, even
        mine, theirs = jnp.where(is_odd, odd, even), jnp.where(is_odd, even, odd)
        places[name] = [me ^ mine ^ entry for entry in share]
        places["core_" + name] = [core ^ theirs ^ entry for entry in share]
    return places


def entry_count(size):
    return 1 << len(far_steps(size))


FIRST = (1, ((7, 7), (5, 5), (3, 3)), True)
SECOND = (1, ((7, 7), (5, 5), (3, 3)), False)
NAMES = ("own", "core", "one", "two", "three", "core_one", "core_two", "core_three")


def fisher_kernel(size, *refs):
    part_refs, (fisher_ref, out_ref, whole_ref) = refs[:-3], refs[-3:]
    layers, rows, feats = fisher_ref.shape
    tiles = feats // LANES
    queries = whole_ref.shape[2]
    places_of = owners(size, FIRST)
    for ref, name in zip(part_refs, NAMES):
        for entry, place in enumerate(places_of[name]):
            whole_ref[place] = ref[entry]
    parts = []
    for layer in range(layers):
        grads = jnp.concatenate(
            [
                whole_ref[:, layer * tiles + tile].reshape(size * queries, LANES)
                for tile in range(tiles)
            ],
            axis=1,
        )
        parts.append(
            lax.dot_general(
                fisher_ref[layer],
                grads,
                (((1,), (1,)), ((), ())),
                preferred_element_type=jnp.float32,
            )
        )
    pieces = [
        part[start : start + LANES] for start in range(0, rows, LANES) for part in parts
    ]
    out_ref[...] = jnp.concatenate(pieces, axis=1).astype(jnp.bfloat16)


def fisher_call(got, inv_fisher, size):
    chunk_shape = got["own"].shape[1:]
    return pl.pallas_call(
        functools.partial(fisher_kernel, size),
        out_shape=jax.ShapeDtypeStruct((LANES, LANES), jnp.bfloat16),
        in_specs=[IN_VMEM] * (len(NAMES) + 1),
        out_specs=IN_VMEM,
        scratch_shapes=[pltpu.VMEM((size,) + chunk_shape, jnp.bfloat16)],
        compiler_params=PARAMS,
    )(*[got[name] for name in NAMES], inv_fisher)


def products(chunk_refs, store_ref, start, total):
    _, count, layers, width = store_ref.shape
    groups = width // LANES
    span = LANES // groups
    lane = lax.broadcasted_iota(jnp.int32, (LANES, LANES), 1)
    for ref in chunk_refs:
        for entry in range(ref.shape[0]):
            chunk = ref[entry]
            weights = jnp.concatenate(
                [
                    jnp.where(lane // span == group, chunk, jnp.zeros_like(chunk))
                    for group in range(groups)
                ],
                axis=0,
            )
            rows = store_ref[start].reshape(count * layers, width)
            start += 1
            product = jnp.dot(rows, weights, preferred_element_type=jnp.float32)
            total = product if total is None else total + product
    return total


def partial_kernel(starts, *refs):
    number = len(starts)
    total = refs[2 * number][...] if len(refs) == 2 * number + 2 else None
    for chunk_ref, store_ref, start in zip(refs, refs[number:], starts):
        total = products([chunk_ref], store_ref, start, total)
    refs[-1][...] = total


def partial_call(chunks, stores, starts, total=None):
    _, count, layers, width = stores[0].shape
    entries = sum(chunk.shape[0] for chunk in chunks)
    flops = 2 * entries * count * layers * width * LANES
    operands = [*chunks, *stores] + ([] if total is None else [total])
    return pl.pallas_call(
        functools.partial(partial_kernel, tuple(starts)),
        out_shape=jax.ShapeDtypeStruct((count * layers, LANES), jnp.float32),
        in_specs=[IN_VMEM] * len(operands),
        out_specs=IN_VMEM,
        cost_estimate=pl.CostEstimate(flops=0, bytes_accessed=0, transcendentals=0),
        compiler_params=PARAMS,
    )(*operands)


def score_kernel(queries, start, *refs):
    *chunk_refs, store_ref, before_ref, scale_ref, out_ref, total_ref = refs
    _, count, layers, width = store_ref.shape
    span = LANES // (width // LANES)
    total_ref[...] = products(chunk_refs, store_ref, start, before_ref[...])
    lane = lax.broadcasted_iota(jnp.int32, (count, LANES), 1)
    mixed = total_ref[pl.ds(0, count, layers)]
    for layer in range(1, layers):
        rows = total_ref[pl.ds(layer, count, layers)]
        mixed = jnp.where(lane % span // queries == layer, rows, mixed)
    turned = mixed.T
    result = turned[:queries]
    for first in range(queries, LANES, queries):
        result = result + turned[first : first + queries]
    out_ref[...] = result * scale_ref[...]


def score_call(chunks, store, start, total, scaling, queries):
    _, count, layers, _ = store.shape
    return pl.pallas_call(
        functools.partial(score_kernel, queries, start),
        out_shape=jax.ShapeDtypeStruct((queries, count), jnp.float32),
        in_specs=[IN_VMEM] * (len(chunks) + 3),
        out_specs=IN_VMEM,
        scratch_shapes=[pltpu.VMEM(total.shape, jnp.float32)],
        compiler_params=PARAMS,
    )(*chunks, store, total, scaling[None, :])


def fits(size, factors, store, inv_fisher):
    queries, layers, _, width = factors.shape
    _, rows, feats = inv_fisher.shape
    return (
        size >= 16
        and size & (size - 1) == 0
        and width == LANES
        and queries == 2
        and layers == 2
        and rows % LANES == 0
        and (rows // LANES) * layers * queries * size == LANES
        and store.shape[0] % LANES == 0
        and feats == rows * size
    )


def solution(mesh):
    size = mesh.shape["blk"]

    def local(factors, token_mask, store, inv_fisher, source_ids, source_weight):
        if not fits(size, factors, store, inv_fisher):
            return plain(factors, token_mask, store, inv_fisher, source_ids, source_weight)
        scaling = make_scaling(source_ids, source_weight)
        grads = grads_call(factors, token_mask)
        ready = {}

        def keep(name, value):
            ready[name] = value
            return value

        def load(name, parts, after):
            return keep(name, load_store(store, size, parts, after))

        homes = (
            ("own", "core"),
            ("one", "core_one"),
            ("two", "three"),
            ("core_two", "core_three"),
        )

        def home_of(name):
            return next(k for k, home in enumerate(homes) if name in home)

        def start_of(name):
            return homes[home_of(name)].index(name) * entry_count(size)

        got = gather(
            grads,
            size,
            FIRST,
            lambda share: [keep("fisher", load_whole(inv_fisher, share))],
            lambda got: [load(0, homes[0], got["own"])],
            lambda got: [load(1, homes[1], got["one"])],
        )
        hidden = fisher_call(got, ready["fisher"], size)

        def add(got, *names):
            total = partial_call(
                [got[name] for name in names],
                [ready[home_of(name)] for name in names],
                [start_of(name) for name in names],
                ready.get("total"),
            )
            return keep("total", total)

        got = gather(
            hidden,
            size,
            SECOND,
            lambda share: [load(2, homes[2], share)],
            lambda got: [add(got, "own", "core"), load(3, homes[3], got["core"])],
            lambda got: [add(got, "one")],
        )
        add(got, "core_one", "two", "three")
        return score_call(
            [got["core_two"], got["core_three"]], ready[3], start_of("core_two"),
            ready["total"], scaling, factors.shape[0] * size,
        )

    placed = (
        P(("groups", "blk"), None, None, None),
        P(("groups", "blk"), None),
        P(("groups", "blk"), None, None),
        P(None, "blk", None),
        P(("groups", "blk")),
        P(),
    )
    return jax.shard_map(
        local, mesh=mesh, in_specs=placed, out_specs=P("groups", "blk"), check_vma=False
    )
```

```python
import functools
import math

import jax
import jax.numpy as jnp
from jax import lax
from jax.experimental import pallas as pl
from jax.experimental.pallas import tpu as pltpu
from jax.sharding import PartitionSpec as P

LANES = 128
IN_VMEM = pl.BlockSpec(memory_space=pltpu.VMEM)
IN_HBM = pl.BlockSpec(memory_space=pltpu.HBM)
PARAMS = pltpu.CompilerParams(vmem_limit_bytes=16 * 2**20)


def make_grads(factors, token_mask):
    rank_size = factors.shape[3] // 2
    mask_values = token_mask.astype(jnp.float32)[:, None, :, None]
    left_side = factors[..., :rank_size].astype(jnp.float32) * mask_values
    right_side = factors[..., rank_size:].astype(jnp.float32)
    outer_sum = jnp.einsum("qlta,qltb->qlab", left_side, right_side)
    return outer_sum.reshape(outer_sum.shape[0], outer_sum.shape[1], rank_size * rank_size).astype(
        jnp.bfloat16
    )


def make_scaling(source_ids, source_weight):
    matches = (
        source_ids[:, None] == jnp.arange(source_weight.shape[0], dtype=jnp.int32)[None, :]
    ).astype(jnp.float32)
    return jnp.sum(matches * source_weight[None, :], axis=1)


def plain(factors, token_mask, store, inv_fisher, source_ids, source_weight):
    segment = lax.all_gather(make_grads(factors, token_mask), "blk", axis=0, tiled=True)
    products = [
        lax.dot_general(
            segment[:, layer_idx],
            inv_fisher[layer_idx],
            (((1,), (1,)), ((), ())),
            preferred_element_type=jnp.float32,
        )
        for layer_idx in range(inv_fisher.shape[0])
    ]
    hidden_cols = jnp.stack(products, axis=1).astype(jnp.bfloat16)
    hidden = lax.all_gather(hidden_cols, "blk", axis=2, tiled=True)
    raw_scores = lax.dot_general(
        hidden, store, (((1, 2), (1, 2)), ((), ())), preferred_element_type=jnp.float32
    )
    return raw_scores * make_scaling(source_ids, source_weight)[None, :]


def zeros_kernel(out_ref):
    out_ref[...] = jnp.zeros_like(out_ref)


def zeros_call(shape):
    return pl.pallas_call(
        zeros_kernel,
        out_shape=jax.ShapeDtypeStruct(shape, jnp.float32),
        out_specs=IN_VMEM,
        cost_estimate=pl.CostEstimate(flops=10**10, bytes_accessed=0, transcendentals=0),
        compiler_params=PARAMS,
    )()


def grads_kernel(factors_ref, mask_ref, zeros_ref, out_ref, outer_ref, flat_ref):
    queries, layers, _, width = factors_ref.shape
    rank = width // 2
    tiles = rank * rank // LANES
    for layer in range(layers):
        for query in range(queries):
            block = factors_ref[query, layer].astype(jnp.float32)
            left = block[:, :rank].T * mask_ref[query : query + 1].astype(jnp.float32)
            outer_ref[...] = zeros_ref[...] + jnp.dot(
                left.astype(jnp.bfloat16),
                block[:, rank:].astype(jnp.bfloat16),
                preferred_element_type=jnp.float32,
            )
            flat_ref[layer, pl.ds(query, tiles, queries)] = jnp.concatenate(
                [outer_ref[pl.ds(0, tiles, 2)], outer_ref[pl.ds(1, tiles, 2)]], axis=1
            )
    out_ref[...] = (
        flat_ref[...].astype(jnp.bfloat16).reshape(layers * tiles, queries, LANES)
    )


def grads_call(factors, token_mask):
    queries, layers, _, width = factors.shape
    rank = width // 2
    tiles = rank * rank // LANES
    return pl.pallas_call(
        grads_kernel,
        out_shape=jax.ShapeDtypeStruct((layers * tiles, queries, LANES), jnp.bfloat16),
        grid=(1,),
        in_specs=[
            pl.BlockSpec(factors.shape, lambda i: (0, 0, 0, 0)),
            pl.BlockSpec(token_mask.shape, lambda i: (0, 0)),
            IN_VMEM,
        ],
        out_specs=pl.BlockSpec((layers * tiles, queries, LANES), lambda i: (0, 0, 0)),
        scratch_shapes=[
            pltpu.VMEM((rank, rank), jnp.float32),
            pltpu.VMEM((layers, tiles * queries, LANES), jnp.float32),
        ],
        cost_estimate=pl.CostEstimate(flops=10**10, bytes_accessed=0, transcendentals=0),
        compiler_params=PARAMS,
    )(factors, token_mask, zeros_call((rank, rank)))


def load_kernel(size, names, source_ref, out_ref, sem):
    width = out_ref.shape[-1]
    places = owners(size, SECOND)
    for entry, owner in enumerate(sum([places[name] for name in names], [])):
        columns = pl.ds(pl.multiple_of(owner * width, width), width)
        pltpu.make_async_copy(source_ref.at[:, :, columns], out_ref.at[entry], sem).start()
    pltpu.make_async_copy(out_ref, out_ref, sem).wait()


def load_store(store, size, names, after):
    store, _ = lax.optimization_barrier((store, after))
    rows, layers, feats = store.shape
    entries = len(names) * entry_count(size)
    shape = (entries, rows, layers, feats // size)
    return pl.pallas_call(
        functools.partial(load_kernel, size, names),
        out_shape=jax.ShapeDtypeStruct(shape, store.dtype),
        in_specs=[IN_HBM],
        out_specs=IN_VMEM,
        scratch_shapes=[pltpu.SemaphoreType.DMA],
        cost_estimate=pl.CostEstimate(
            flops=0, bytes_accessed=2 * math.prod(shape), transcendentals=0
        ),
        compiler_params=PARAMS,
    )(store)


def copy_kernel(source_ref, out_ref, sem):
    copy = pltpu.make_async_copy(source_ref, out_ref, sem)
    copy.start()
    copy.wait()


def load_whole(source, after):
    source, _ = lax.optimization_barrier((source, after))
    return pl.pallas_call(
        copy_kernel,
        out_shape=jax.ShapeDtypeStruct(source.shape, source.dtype),
        in_specs=[IN_HBM],
        out_specs=IN_VMEM,
        scratch_shapes=[pltpu.SemaphoreType.DMA],
        cost_estimate=pl.CostEstimate(
            flops=0, bytes_accessed=2 * source.size, transcendentals=0
        ),
        compiler_params=PARAMS,
    )(source)


def send(value, even, odd, size):
    pairs = [(i, i ^ (odd if i % 2 else even)) for i in range(size)]
    return lax.ppermute(value, "blk", pairs)


def far_steps(size):
    return [size >> k for k in range(1, size.bit_length()) if size >> k > 4]


def gather(chunk, size, plan, early, middle, late):
    flip, square, late_core = plan
    share = chunk[None]
    for step in far_steps(size):
        other = send(share, step ^ flip, step ^ flip, size)
        if step == size // 2:
            other, *_ = lax.optimization_barrier((other, *early(share)))
        share = jnp.concatenate([share, other], axis=0)
    one, two, three = (send(share, even, odd, size) for even, odd in square)
    got = {"own": share}
    if late_core:
        one, *_ = lax.optimization_barrier((one, *middle(got)))
        held, _ = lax.optimization_barrier((share, one))
        got["core"] = send(held, 1, 1, size)
    else:
        got["core"] = send(share, 1, 1, size)
        one, got["core"], *_ = lax.optimization_barrier((one, got["core"], *middle(got)))
    got.update(one=one, core_one=send(one, 1, 1, size))
    two, three, *_ = lax.optimization_barrier(
        (two, three, got["core"], got["core_one"], *late(got))
    )
    got.update(two=two, core_two=send(two, 1, 1, size))
    got.update(three=three, core_three=send(three, 1, 1, size))
    return got


def owners(size, plan):
    me = lax.axis_index("blk")
    core = me ^ 1
    is_odd = lax.rem(me, 2) == 1
    share = [0]
    for step in far_steps(size):
        share = share + [step ^ plan[0] ^ entry for entry in share]
    places = {"own": [me ^ entry for entry in share], "core": [core ^ entry for entry in share]}
    for name, (even, odd) in zip(("one", "two", "three"), plan[1]):
        if even % 2:
            even, odd = odd, even
        mine, theirs = jnp.where(is_odd, odd, even), jnp.where(is_odd, even, odd)
        places[name] = [me ^ mine ^ entry for entry in share]
        places["core_" + name] = [core ^ theirs ^ entry for entry in share]
    return places


def entry_count(size):
    return 1 << len(far_steps(size))


FIRST = (1, ((7, 7), (5, 5), (3, 3)), True)
SECOND = (1, ((7, 7), (5, 5), (3, 3)), False)
NAMES = ("own", "core", "one", "two", "three", "core_one", "core_two", "core_three")


def fisher_kernel(size, *refs):
    part_refs, (fisher_ref, out_ref, whole_ref) = refs[:-3], refs[-3:]
    layers, rows, feats = fisher_ref.shape
    tiles = feats // LANES
    queries = whole_ref.shape[2]
    places_of = owners(size, FIRST)
    for ref, name in zip(part_refs, NAMES):
        for entry, place in enumerate(places_of[name]):
            whole_ref[place] = ref[entry]
    parts = []
    for layer in range(layers):
        grads = jnp.concatenate(
            [
                whole_ref[:, layer * tiles + tile].reshape(size * queries, LANES)
                for tile in range(tiles)
            ],
            axis=1,
        )
        parts.append(
            lax.dot_general(
                fisher_ref[layer],
                grads,
                (((1,), (1,)), ((), ())),
                preferred_element_type=jnp.float32,
            )
        )
    pieces = [
        part[start : start + LANES] for start in range(0, rows, LANES) for part in parts
    ]
    out_ref[...] = jnp.concatenate(pieces, axis=1).astype(jnp.bfloat16)


def fisher_call(got, inv_fisher, size):
    chunk_shape = got["own"].shape[1:]
    return pl.pallas_call(
        functools.partial(fisher_kernel, size),
        out_shape=jax.ShapeDtypeStruct((LANES, LANES), jnp.bfloat16),
        in_specs=[IN_VMEM] * (len(NAMES) + 1),
        out_specs=IN_VMEM,
        scratch_shapes=[pltpu.VMEM((size,) + chunk_shape, jnp.bfloat16)],
        compiler_params=PARAMS,
    )(*[got[name] for name in NAMES], inv_fisher)


def products(chunk_refs, store_ref, start, total):
    _, count, layers, width = store_ref.shape
    groups = width // LANES
    span = LANES // groups
    lane = lax.broadcasted_iota(jnp.int32, (LANES, LANES), 1)
    for ref in chunk_refs:
        for entry in range(ref.shape[0]):
            chunk = ref[entry]
            weights = jnp.concatenate(
                [
                    jnp.where(lane // span == group, chunk, jnp.zeros_like(chunk))
                    for group in range(groups)
                ],
                axis=0,
            )
            rows = store_ref[start].reshape(count * layers, width)
            start += 1
            product = jnp.dot(rows, weights, preferred_element_type=jnp.float32)
            total = product if total is None else total + product
    return total


def partial_kernel(starts, *refs):
    number = len(starts)
    total = refs[2 * number][...] if len(refs) == 2 * number + 2 else None
    for chunk_ref, store_ref, start in zip(refs, refs[number:], starts):
        total = products([chunk_ref], store_ref, start, total)
    refs[-1][...] = total


def partial_call(chunks, stores, starts, total=None):
    _, count, layers, width = stores[0].shape
    entries = sum(chunk.shape[0] for chunk in chunks)
    flops = 2 * entries * count * layers * width * LANES
    operands = [*chunks, *stores] + ([] if total is None else [total])
    return pl.pallas_call(
        functools.partial(partial_kernel, tuple(starts)),
        out_shape=jax.ShapeDtypeStruct((count * layers, LANES), jnp.float32),
        in_specs=[IN_VMEM] * len(operands),
        out_specs=IN_VMEM,
        cost_estimate=pl.CostEstimate(flops=0, bytes_accessed=0, transcendentals=0),
        compiler_params=PARAMS,
    )(*operands)


def score_kernel(queries, start, *refs):
    *chunk_refs, store_ref, before_ref, scale_ref, out_ref, total_ref = refs
    _, count, layers, width = store_ref.shape
    span = LANES // (width // LANES)
    total_ref[...] = products(chunk_refs, store_ref, start, before_ref[...])
    lane = lax.broadcasted_iota(jnp.int32, (count, LANES), 1)
    mixed = total_ref[pl.ds(0, count, layers)]
    for layer in range(1, layers):
        rows = total_ref[pl.ds(layer, count, layers)]
        mixed = jnp.where(lane % span // queries == layer, rows, mixed)
    turned = mixed.T
    result = turned[:queries]
    for first in range(queries, LANES, queries):
        result = result + turned[first : first + queries]
    out_ref[...] = result * scale_ref[...]


def score_call(chunks, store, start, total, scaling, queries):
    _, count, layers, _ = store.shape
    return pl.pallas_call(
        functools.partial(score_kernel, queries, start),
        out_shape=jax.ShapeDtypeStruct((queries, count), jnp.float32),
        in_specs=[IN_VMEM] * (len(chunks) + 3),
        out_specs=IN_VMEM,
        scratch_shapes=[pltpu.VMEM(total.shape, jnp.float32)],
        compiler_params=PARAMS,
    )(*chunks, store, total, scaling[None, :])


def fits(size, factors, store, inv_fisher):
    queries, layers, _, width = factors.shape
    _, rows, feats = inv_fisher.shape
    return (
        size >= 16
        and size & (size - 1) == 0
        and width == LANES
        and queries == 2
        and layers == 2
        and rows % LANES == 0
        and (rows // LANES) * layers * queries * size == LANES
        and store.shape[0] % LANES == 0
        and feats == rows * size
    )


def solution(mesh):
    size = mesh.shape["blk"]

    def local(factors, token_mask, store, inv_fisher, source_ids, source_weight):
        if not fits(size, factors, store, inv_fisher):
            return plain(factors, token_mask, store, inv_fisher, source_ids, source_weight)
        scaling = make_scaling(source_ids, source_weight)
        grads = grads_call(factors, token_mask)
        ready = {}

        def keep(name, value):
            ready[name] = value
            return value

        def load(name, parts, after):
            return keep(name, load_store(store, size, parts, after))

        homes = (
            ("own", "core"),
            ("one", "core_one"),
            ("two", "three"),
            ("core_two", "core_three"),
        )

        def home_of(name):
            return next(k for k, home in enumerate(homes) if name in home)

        def start_of(name):
            return homes[home_of(name)].index(name) * entry_count(size)

        got = gather(
            grads,
            size,
            FIRST,
            lambda share: [keep("fisher", load_whole(inv_fisher, share))],
            lambda got: [load(0, homes[0], got["own"])],
            lambda got: [load(1, homes[1], got["one"])],
        )
        hidden = fisher_call(got, ready["fisher"], size)

        def add(got, *names):
            total = partial_call(
                [got[name] for name in names],
                [ready[home_of(name)] for name in names],
                [start_of(name) for name in names],
                ready.get("total"),
            )
            return keep("total", total)

        got = gather(
            hidden,
            size,
            SECOND,
            lambda share: [load(2, homes[2], share)],
            lambda got: [add(got, "own", "core"), load(3, homes[3], got["core"])],
            lambda got: [add(got, "one")],
        )
        add(got, "core_one", "two", "three")
        return score_call(
            [got["core_two"], got["core_three"]], ready[3], start_of("core_two"),
            ready["total"], scaling, factors.shape[0] * size,
        )

    placed = (
        P(("groups", "blk"), None, None, None),
        P(("groups", "blk"), None),
        P(("groups", "blk"), None, None),
        P(None, "blk", None),
        P(("groups", "blk")),
        P(),
    )
    return jax.shard_map(
        local, mesh=mesh, in_specs=placed, out_specs=P("groups", "blk"), check_vma=False
    )
```

```python
import functools
import math

import jax
import jax.numpy as jnp
from jax import lax
from jax.experimental import pallas as pl
from jax.experimental.pallas import tpu as pltpu
from jax.sharding import PartitionSpec as P

LANES = 128
IN_VMEM = pl.BlockSpec(memory_space=pltpu.VMEM)
IN_HBM = pl.BlockSpec(memory_space=pltpu.HBM)
PARAMS = pltpu.CompilerParams(vmem_limit_bytes=16 * 2**20)


def make_grads(factors, token_mask):
    rank_size = factors.shape[3] // 2
    mask_values = token_mask.astype(jnp.float32)[:, None, :, None]
    left_side = factors[..., :rank_size].astype(jnp.float32) * mask_values
    right_side = factors[..., rank_size:].astype(jnp.float32)
    outer_sum = jnp.einsum("qlta,qltb->qlab", left_side, right_side)
    return outer_sum.reshape(outer_sum.shape[0], outer_sum.shape[1], rank_size * rank_size).astype(
        jnp.bfloat16
    )


def make_scaling(source_ids, source_weight):
    matches = (
        source_ids[:, None] == jnp.arange(source_weight.shape[0], dtype=jnp.int32)[None, :]
    ).astype(jnp.float32)
    return jnp.sum(matches * source_weight[None, :], axis=1)


def plain(factors, token_mask, store, inv_fisher, source_ids, source_weight):
    segment = lax.all_gather(make_grads(factors, token_mask), "blk", axis=0, tiled=True)
    products = [
        lax.dot_general(
            segment[:, layer_idx],
            inv_fisher[layer_idx],
            (((1,), (1,)), ((), ())),
            preferred_element_type=jnp.float32,
        )
        for layer_idx in range(inv_fisher.shape[0])
    ]
    hidden_cols = jnp.stack(products, axis=1).astype(jnp.bfloat16)
    hidden = lax.all_gather(hidden_cols, "blk", axis=2, tiled=True)
    raw_scores = lax.dot_general(
        hidden, store, (((1, 2), (1, 2)), ((), ())), preferred_element_type=jnp.float32
    )
    return raw_scores * make_scaling(source_ids, source_weight)[None, :]


def zeros_kernel(out_ref):
    out_ref[...] = jnp.zeros_like(out_ref)


def zeros_call(shape):
    return pl.pallas_call(
        zeros_kernel,
        out_shape=jax.ShapeDtypeStruct(shape, jnp.float32),
        out_specs=IN_VMEM,
        cost_estimate=pl.CostEstimate(flops=10**10, bytes_accessed=0, transcendentals=0),
        compiler_params=PARAMS,
    )()


def grads_kernel(factors_ref, mask_ref, zeros_ref, out_ref, outer_ref, flat_ref):
    queries, layers, _, width = factors_ref.shape
    rank = width // 2
    tiles = rank * rank // LANES
    for layer in range(layers):
        for query in range(queries):
            block = factors_ref[query, layer].astype(jnp.float32)
            left = block[:, :rank].T * mask_ref[query : query + 1].astype(jnp.float32)
            outer_ref[...] = zeros_ref[...] + jnp.dot(
                left.astype(jnp.bfloat16),
                block[:, rank:].astype(jnp.bfloat16),
                preferred_element_type=jnp.float32,
            )
            flat_ref[layer, pl.ds(query, tiles, queries)] = jnp.concatenate(
                [outer_ref[pl.ds(0, tiles, 2)], outer_ref[pl.ds(1, tiles, 2)]], axis=1
            )
    out_ref[...] = (
        flat_ref[...].astype(jnp.bfloat16).reshape(layers * tiles, queries, LANES)
    )


def grads_call(factors, token_mask):
    queries, layers, _, width = factors.shape
    rank = width // 2
    tiles = rank * rank // LANES
    return pl.pallas_call(
        grads_kernel,
        out_shape=jax.ShapeDtypeStruct((layers * tiles, queries, LANES), jnp.bfloat16),
        grid=(1,),
        in_specs=[
            pl.BlockSpec(factors.shape, lambda i: (0, 0, 0, 0)),
            pl.BlockSpec(token_mask.shape, lambda i: (0, 0)),
            IN_VMEM,
        ],
        out_specs=pl.BlockSpec((layers * tiles, queries, LANES), lambda i: (0, 0, 0)),
        scratch_shapes=[
            pltpu.VMEM((rank, rank), jnp.float32),
            pltpu.VMEM((layers, tiles * queries, LANES), jnp.float32),
        ],
        cost_estimate=pl.CostEstimate(flops=10**10, bytes_accessed=0, transcendentals=0),
        compiler_params=PARAMS,
    )(factors, token_mask, zeros_call((rank, rank)))


def load_kernel(size, names, source_ref, out_ref, sem):
    width = out_ref.shape[-1]
    places = owners(size, SECOND)
    for entry, owner in enumerate(sum([places[name] for name in names], [])):
        columns = pl.ds(pl.multiple_of(owner * width, width), width)
        pltpu.make_async_copy(source_ref.at[:, :, columns], out_ref.at[entry], sem).start()
    pltpu.make_async_copy(out_ref, out_ref, sem).wait()


def load_store(store, size, names, after):
    store, _ = lax.optimization_barrier((store, after))
    rows, layers, feats = store.shape
    entries = sum(entry_count(name, size) for name in names)
    shape = (entries, rows, layers, feats // size)
    return pl.pallas_call(
        functools.partial(load_kernel, size, names),
        out_shape=jax.ShapeDtypeStruct(shape, store.dtype),
        in_specs=[IN_HBM],
        out_specs=IN_VMEM,
        scratch_shapes=[pltpu.SemaphoreType.DMA],
        cost_estimate=pl.CostEstimate(
            flops=0, bytes_accessed=2 * math.prod(shape), transcendentals=0
        ),
        compiler_params=PARAMS,
    )(store)


def copy_kernel(source_ref, out_ref, sem):
    copy = pltpu.make_async_copy(source_ref, out_ref, sem)
    copy.start()
    copy.wait()


def load_whole(source, after):
    source, _ = lax.optimization_barrier((source, after))
    return pl.pallas_call(
        copy_kernel,
        out_shape=jax.ShapeDtypeStruct(source.shape, source.dtype),
        in_specs=[IN_HBM],
        out_specs=IN_VMEM,
        scratch_shapes=[pltpu.SemaphoreType.DMA],
        cost_estimate=pl.CostEstimate(
            flops=0, bytes_accessed=2 * source.size, transcendentals=0
        ),
        compiler_params=PARAMS,
    )(source)


def send(value, even, odd, size):
    pairs = [(i, i ^ (odd if i % 2 else even)) for i in range(size)]
    return lax.ppermute(value, "blk", pairs)


def far_steps(size):
    return [size >> k for k in range(1, size.bit_length()) if size >> k > 4]


def gather(chunk, size, plan, early, middle, late):
    flip, square, late_core = plan
    share = chunk[None]
    for step in far_steps(size):
        other = send(share, step ^ flip, step ^ flip, size)
        if step == size // 2:
            other, *_ = lax.optimization_barrier((other, *early(share)))
        share = jnp.concatenate([share, other], axis=0)
    one, two, three = (send(share, even, odd, size) for even, odd in square)
    got = {"own": share}
    if late_core:
        one, *_ = lax.optimization_barrier((one, *middle(got)))
        held, _ = lax.optimization_barrier((share, one))
        got["core"] = send(held, 1, 1, size)
    else:
        got["core"] = send(share, 1, 1, size)
        one, got["core"], *_ = lax.optimization_barrier((one, got["core"], *middle(got)))
    got.update(one=one, core_one=send(one, 1, 1, size))
    two, three, *_ = lax.optimization_barrier(
        (two, three, got["core"], got["core_one"], *late(got))
    )
    last = jnp.concatenate([two, three], axis=0)
    got.update(last=last, core_last=send(last, 1, 1, size))
    return got


def owners(size, plan):
    me = lax.axis_index("blk")
    core = me ^ 1
    is_odd = lax.rem(me, 2) == 1
    share = [0]
    for step in far_steps(size):
        share = share + [step ^ plan[0] ^ entry for entry in share]
    places = {"own": [me ^ entry for entry in share], "core": [core ^ entry for entry in share]}
    for name, (even, odd) in zip(("one", "two", "three"), plan[1]):
        if even % 2:
            even, odd = odd, even
        mine, theirs = jnp.where(is_odd, odd, even), jnp.where(is_odd, even, odd)
        places[name] = [me ^ mine ^ entry for entry in share]
        places["core_" + name] = [core ^ theirs ^ entry for entry in share]
    for name in ("", "core_"):
        places[name + "last"] = places.pop(name + "two") + places.pop(name + "three")
    return places


def entry_count(name, size):
    return (2 if name.endswith("last") else 1) << len(far_steps(size))


FIRST = (1, ((7, 7), (5, 5), (3, 3)), True)
SECOND = (1, ((7, 7), (5, 5), (3, 3)), False)
NAMES = ("own", "core", "one", "core_one", "last", "core_last")


def fisher_kernel(size, *refs):
    part_refs, (fisher_ref, out_ref, whole_ref) = refs[:-3], refs[-3:]
    layers, rows, feats = fisher_ref.shape
    tiles = feats // LANES
    queries = whole_ref.shape[2]
    places_of = owners(size, FIRST)
    for ref, name in zip(part_refs, NAMES):
        for entry, place in enumerate(places_of[name]):
            whole_ref[place] = ref[entry]
    parts = []
    for layer in range(layers):
        grads = jnp.concatenate(
            [
                whole_ref[:, layer * tiles + tile].reshape(size * queries, LANES)
                for tile in range(tiles)
            ],
            axis=1,
        )
        parts.append(
            lax.dot_general(
                fisher_ref[layer],
                grads,
                (((1,), (1,)), ((), ())),
                preferred_element_type=jnp.float32,
            )
        )
    pieces = [
        part[start : start + LANES] for start in range(0, rows, LANES) for part in parts
    ]
    out_ref[...] = jnp.concatenate(pieces, axis=1).astype(jnp.bfloat16)


def fisher_call(got, inv_fisher, size):
    chunk_shape = got["own"].shape[1:]
    return pl.pallas_call(
        functools.partial(fisher_kernel, size),
        out_shape=jax.ShapeDtypeStruct((LANES, LANES), jnp.bfloat16),
        in_specs=[IN_VMEM] * (len(NAMES) + 1),
        out_specs=IN_VMEM,
        scratch_shapes=[pltpu.VMEM((size,) + chunk_shape, jnp.bfloat16)],
        compiler_params=PARAMS,
    )(*[got[name] for name in NAMES], inv_fisher)


def products(chunk_refs, store_ref, start, total):
    _, count, layers, width = store_ref.shape
    groups = width // LANES
    span = LANES // groups
    lane = lax.broadcasted_iota(jnp.int32, (LANES, LANES), 1)
    for ref in chunk_refs:
        for entry in range(ref.shape[0]):
            chunk = ref[entry]
            weights = jnp.concatenate(
                [
                    jnp.where(lane // span == group, chunk, jnp.zeros_like(chunk))
                    for group in range(groups)
                ],
                axis=0,
            )
            rows = store_ref[start].reshape(count * layers, width)
            start += 1
            product = jnp.dot(rows, weights, preferred_element_type=jnp.float32)
            total = product if total is None else total + product
    return total


def partial_kernel(starts, *refs):
    number = len(starts)
    total = refs[2 * number][...] if len(refs) == 2 * number + 2 else None
    for chunk_ref, store_ref, start in zip(refs, refs[number:], starts):
        total = products([chunk_ref], store_ref, start, total)
    refs[-1][...] = total


def partial_call(chunks, stores, starts, total=None):
    _, count, layers, width = stores[0].shape
    entries = sum(chunk.shape[0] for chunk in chunks)
    flops = 2 * entries * count * layers * width * LANES
    operands = [*chunks, *stores] + ([] if total is None else [total])
    return pl.pallas_call(
        functools.partial(partial_kernel, tuple(starts)),
        out_shape=jax.ShapeDtypeStruct((count * layers, LANES), jnp.float32),
        in_specs=[IN_VMEM] * len(operands),
        out_specs=IN_VMEM,
        cost_estimate=pl.CostEstimate(flops=0, bytes_accessed=0, transcendentals=0),
        compiler_params=PARAMS,
    )(*operands)


def score_kernel(queries, start, *refs):
    *chunk_refs, store_ref, before_ref, scale_ref, out_ref, total_ref = refs
    _, count, layers, width = store_ref.shape
    span = LANES // (width // LANES)
    total_ref[...] = products(chunk_refs, store_ref, start, before_ref[...])
    lane = lax.broadcasted_iota(jnp.int32, (count, LANES), 1)
    mixed = total_ref[pl.ds(0, count, layers)]
    for layer in range(1, layers):
        rows = total_ref[pl.ds(layer, count, layers)]
        mixed = jnp.where(lane % span // queries == layer, rows, mixed)
    turned = mixed.T
    result = turned[:queries]
    for first in range(queries, LANES, queries):
        result = result + turned[first : first + queries]
    out_ref[...] = result * scale_ref[...]


def score_call(chunks, store, start, total, scaling, queries):
    _, count, layers, _ = store.shape
    return pl.pallas_call(
        functools.partial(score_kernel, queries, start),
        out_shape=jax.ShapeDtypeStruct((queries, count), jnp.float32),
        in_specs=[IN_VMEM] * (len(chunks) + 3),
        out_specs=IN_VMEM,
        scratch_shapes=[pltpu.VMEM(total.shape, jnp.float32)],
        compiler_params=PARAMS,
    )(*chunks, store, total, scaling[None, :])


def fits(size, factors, store, inv_fisher):
    queries, layers, _, width = factors.shape
    _, rows, feats = inv_fisher.shape
    return (
        size >= 16
        and size & (size - 1) == 0
        and width == LANES
        and queries == 2
        and layers == 2
        and rows % LANES == 0
        and (rows // LANES) * layers * queries * size == LANES
        and store.shape[0] % LANES == 0
        and feats == rows * size
    )


def solution(mesh):
    size = mesh.shape["blk"]

    def local(factors, token_mask, store, inv_fisher, source_ids, source_weight):
        if not fits(size, factors, store, inv_fisher):
            return plain(factors, token_mask, store, inv_fisher, source_ids, source_weight)
        scaling = make_scaling(source_ids, source_weight)
        grads = grads_call(factors, token_mask)
        ready = {}

        def keep(name, value):
            ready[name] = value
            return value

        def load(name, parts, after):
            return keep(name, load_store(store, size, parts, after))

        homes = (
            ("own", "core"),
            ("one", "core_one"),
            ("last",),
            ("core_last",),
        )

        def home_of(name):
            return next(k for k, home in enumerate(homes) if name in home)

        def start_of(name):
            home = homes[home_of(name)]
            return sum(entry_count(other, size) for other in home[: home.index(name)])

        got = gather(
            grads,
            size,
            FIRST,
            lambda share: [keep("fisher", load_whole(inv_fisher, share))],
            lambda got: [load(0, homes[0], got["own"])],
            lambda got: [load(1, homes[1], got["one"])],
        )
        hidden = fisher_call(got, ready["fisher"], size)

        def add(got, *names):
            total = partial_call(
                [got[name] for name in names],
                [ready[home_of(name)] for name in names],
                [start_of(name) for name in names],
                ready.get("total"),
            )
            return keep("total", total)

        got = gather(
            hidden,
            size,
            SECOND,
            lambda share: [load(2, homes[2], share)],
            lambda got: [add(got, "own", "core"), load(3, homes[3], got["core"])],
            lambda got: [add(got, "one")],
        )
        add(got, "core_one", "last")
        return score_call(
            [got["core_last"]], ready[3], start_of("core_last"),
            ready["total"], scaling, factors.shape[0] * size,
        )

    placed = (
        P(("groups", "blk"), None, None, None),
        P(("groups", "blk"), None),
        P(("groups", "blk"), None, None),
        P(None, "blk", None),
        P(("groups", "blk")),
        P(),
    )
    return jax.shard_map(
        local, mesh=mesh, in_specs=placed, out_specs=P("groups", "blk"), check_vma=False
    )
```

```python
import functools
import math

import jax
import jax.numpy as jnp
from jax import lax
from jax.experimental import pallas as pl
from jax.experimental.pallas import tpu as pltpu
from jax.sharding import PartitionSpec as P

LANES = 128
IN_VMEM = pl.BlockSpec(memory_space=pltpu.VMEM)
IN_HBM = pl.BlockSpec(memory_space=pltpu.HBM)
PARAMS = pltpu.CompilerParams(vmem_limit_bytes=16 * 2**20)


def make_grads(factors, token_mask):
    rank_size = factors.shape[3] // 2
    mask_values = token_mask.astype(jnp.float32)[:, None, :, None]
    left_side = factors[..., :rank_size].astype(jnp.float32) * mask_values
    right_side = factors[..., rank_size:].astype(jnp.float32)
    outer_sum = jnp.einsum("qlta,qltb->qlab", left_side, right_side)
    return outer_sum.reshape(outer_sum.shape[0], outer_sum.shape[1], rank_size * rank_size).astype(
        jnp.bfloat16
    )


def make_scaling(source_ids, source_weight):
    matches = (
        source_ids[:, None] == jnp.arange(source_weight.shape[0], dtype=jnp.int32)[None, :]
    ).astype(jnp.float32)
    return jnp.sum(matches * source_weight[None, :], axis=1)


def plain(factors, token_mask, store, inv_fisher, source_ids, source_weight):
    segment = lax.all_gather(make_grads(factors, token_mask), "blk", axis=0, tiled=True)
    products = [
        lax.dot_general(
            segment[:, layer_idx],
            inv_fisher[layer_idx],
            (((1,), (1,)), ((), ())),
            preferred_element_type=jnp.float32,
        )
        for layer_idx in range(inv_fisher.shape[0])
    ]
    hidden_cols = jnp.stack(products, axis=1).astype(jnp.bfloat16)
    hidden = lax.all_gather(hidden_cols, "blk", axis=2, tiled=True)
    raw_scores = lax.dot_general(
        hidden, store, (((1, 2), (1, 2)), ((), ())), preferred_element_type=jnp.float32
    )
    return raw_scores * make_scaling(source_ids, source_weight)[None, :]


def zeros_kernel(out_ref):
    out_ref[...] = jnp.zeros_like(out_ref)


def zeros_call(shape):
    return pl.pallas_call(
        zeros_kernel,
        out_shape=jax.ShapeDtypeStruct(shape, jnp.float32),
        out_specs=IN_VMEM,
        cost_estimate=pl.CostEstimate(flops=10**10, bytes_accessed=0, transcendentals=0),
        compiler_params=PARAMS,
    )()


def grads_kernel(factors_ref, mask_ref, zeros_ref, out_ref, outer_ref, flat_ref):
    queries, layers, _, width = factors_ref.shape
    rank = width // 2
    tiles = rank * rank // LANES
    for layer in range(layers):
        for query in range(queries):
            block = factors_ref[query, layer].astype(jnp.float32)
            left = block[:, :rank].T * mask_ref[query : query + 1].astype(jnp.float32)
            outer_ref[...] = zeros_ref[...] + jnp.dot(
                left.astype(jnp.bfloat16),
                block[:, rank:].astype(jnp.bfloat16),
                preferred_element_type=jnp.float32,
            )
            flat_ref[layer, pl.ds(query, tiles, queries)] = jnp.concatenate(
                [outer_ref[pl.ds(0, tiles, 2)], outer_ref[pl.ds(1, tiles, 2)]], axis=1
            )
    out_ref[...] = (
        flat_ref[...].astype(jnp.bfloat16).reshape(layers * tiles, queries, LANES)
    )


def grads_call(factors, token_mask):
    queries, layers, _, width = factors.shape
    rank = width // 2
    tiles = rank * rank // LANES
    return pl.pallas_call(
        grads_kernel,
        out_shape=jax.ShapeDtypeStruct((layers * tiles, queries, LANES), jnp.bfloat16),
        grid=(1,),
        in_specs=[
            pl.BlockSpec(factors.shape, lambda i: (0, 0, 0, 0)),
            pl.BlockSpec(token_mask.shape, lambda i: (0, 0)),
            IN_VMEM,
        ],
        out_specs=pl.BlockSpec((layers * tiles, queries, LANES), lambda i: (0, 0, 0)),
        scratch_shapes=[
            pltpu.VMEM((rank, rank), jnp.float32),
            pltpu.VMEM((layers, tiles * queries, LANES), jnp.float32),
        ],
        cost_estimate=pl.CostEstimate(flops=10**10, bytes_accessed=0, transcendentals=0),
        compiler_params=PARAMS,
    )(factors, token_mask, zeros_call((rank, rank)))


def load_kernel(size, names, source_ref, out_ref, sem):
    width = out_ref.shape[-1]
    places = owners(size, SECOND)
    for entry, owner in enumerate(sum([places[name] for name in names], [])):
        columns = pl.ds(pl.multiple_of(owner * width, width), width)
        pltpu.make_async_copy(source_ref.at[:, :, columns], out_ref.at[entry], sem).start()
    pltpu.make_async_copy(out_ref, out_ref, sem).wait()


def load_store(store, size, names, after):
    store, _ = lax.optimization_barrier((store, after))
    rows, layers, feats = store.shape
    entries = sum(entry_count(name, size) for name in names)
    shape = (entries, rows, layers, feats // size)
    return pl.pallas_call(
        functools.partial(load_kernel, size, names),
        out_shape=jax.ShapeDtypeStruct(shape, store.dtype),
        in_specs=[IN_HBM],
        out_specs=IN_VMEM,
        scratch_shapes=[pltpu.SemaphoreType.DMA],
        cost_estimate=pl.CostEstimate(
            flops=0, bytes_accessed=2 * math.prod(shape), transcendentals=0
        ),
        compiler_params=PARAMS,
    )(store)


def copy_kernel(source_ref, out_ref, sem):
    copy = pltpu.make_async_copy(source_ref, out_ref, sem)
    copy.start()
    copy.wait()


def load_whole(source, after):
    source, _ = lax.optimization_barrier((source, after))
    return pl.pallas_call(
        copy_kernel,
        out_shape=jax.ShapeDtypeStruct(source.shape, source.dtype),
        in_specs=[IN_HBM],
        out_specs=IN_VMEM,
        scratch_shapes=[pltpu.SemaphoreType.DMA],
        cost_estimate=pl.CostEstimate(
            flops=0, bytes_accessed=2 * source.size, transcendentals=0
        ),
        compiler_params=PARAMS,
    )(source)


def send(value, even, odd, size):
    pairs = [(i, i ^ (odd if i % 2 else even)) for i in range(size)]
    return lax.ppermute(value, "blk", pairs)


def far_steps(size):
    return [size >> k for k in range(1, size.bit_length()) if size >> k > 4]


def gather(chunk, size, plan, early, middle, late):
    flip, square, late_core = plan
    share = chunk[None]
    for step in far_steps(size):
        other = send(share, step ^ flip, step ^ flip, size)
        if step == size // 2:
            other, *_ = lax.optimization_barrier((other, *early(share)))
        share = jnp.concatenate([share, other], axis=0)
    one, two, three = (send(share, even, odd, size) for even, odd in square)
    got = {"own": share}
    if late_core:
        one, *_ = lax.optimization_barrier((one, *middle(got)))
        held, _ = lax.optimization_barrier((share, one))
        got["core"] = send(held, 1, 1, size)
    else:
        got["core"] = send(share, 1, 1, size)
        one, got["core"], *_ = lax.optimization_barrier((one, got["core"], *middle(got)))
    got.update(one=one, core_one=send(one, 1, 1, size))
    two, three, *_ = lax.optimization_barrier(
        (two, three, got["core"], got["core_one"], *late(got))
    )
    last = jnp.concatenate([two, three], axis=0)
    got.update(last=last, core_last=send(last, 1, 1, size))
    return got


def owners(size, plan):
    me = lax.axis_index("blk")
    core = me ^ 1
    is_odd = lax.rem(me, 2) == 1
    share = [0]
    for step in far_steps(size):
        share = share + [step ^ plan[0] ^ entry for entry in share]
    places = {"own": [me ^ entry for entry in share], "core": [core ^ entry for entry in share]}
    for name, (even, odd) in zip(("one", "two", "three"), plan[1]):
        if even % 2:
            even, odd = odd, even
        mine, theirs = jnp.where(is_odd, odd, even), jnp.where(is_odd, even, odd)
        places[name] = [me ^ mine ^ entry for entry in share]
        places["core_" + name] = [core ^ theirs ^ entry for entry in share]
    for name in ("", "core_"):
        places[name + "last"] = places.pop(name + "two") + places.pop(name + "three")
    return places


def entry_count(name, size):
    return (2 if name.endswith("last") else 1) << len(far_steps(size))


FIRST = (1, ((7, 7), (5, 5), (3, 3)), True)
SECOND = (1, ((7, 7), (5, 5), (3, 3)), False)
NAMES = ("own", "core", "one", "core_one", "last", "core_last")


def fisher_kernel(size, *refs):
    part_refs, (fisher_ref, out_ref, whole_ref) = refs[:-3], refs[-3:]
    layers, rows, feats = fisher_ref.shape
    tiles = feats // LANES
    queries = whole_ref.shape[2]
    places_of = owners(size, FIRST)
    for ref, name in zip(part_refs, NAMES):
        for entry, place in enumerate(places_of[name]):
            whole_ref[place] = ref[entry]
    parts = []
    for layer in range(layers):
        grads = jnp.concatenate(
            [
                whole_ref[:, layer * tiles + tile].reshape(size * queries, LANES)
                for tile in range(tiles)
            ],
            axis=1,
        )
        parts.append(
            lax.dot_general(
                fisher_ref[layer],
                grads,
                (((1,), (1,)), ((), ())),
                preferred_element_type=jnp.float32,
            )
        )
    pieces = [
        part[start : start + LANES] for start in range(0, rows, LANES) for part in parts
    ]
    out_ref[...] = jnp.concatenate(pieces, axis=1).astype(jnp.bfloat16)


def fisher_call(got, inv_fisher, size):
    chunk_shape = got["own"].shape[1:]
    return pl.pallas_call(
        functools.partial(fisher_kernel, size),
        out_shape=jax.ShapeDtypeStruct((LANES, LANES), jnp.bfloat16),
        in_specs=[IN_VMEM] * (len(NAMES) + 1),
        out_specs=IN_VMEM,
        scratch_shapes=[pltpu.VMEM((size,) + chunk_shape, jnp.bfloat16)],
        compiler_params=PARAMS,
    )(*[got[name] for name in NAMES], inv_fisher)


def products(chunk_refs, store_ref, start, total):
    _, count, layers, width = store_ref.shape
    groups = width // LANES
    span = LANES // groups
    lane = lax.broadcasted_iota(jnp.int32, (LANES, LANES), 1)
    for ref in chunk_refs:
        for entry in range(ref.shape[0]):
            chunk = ref[entry]
            weights = jnp.concatenate(
                [
                    jnp.where(lane // span == group, chunk, jnp.zeros_like(chunk))
                    for group in range(groups)
                ],
                axis=0,
            )
            rows = store_ref[start].reshape(count * layers, width)
            start += 1
            product = jnp.dot(rows, weights, preferred_element_type=jnp.float32)
            total = product if total is None else total + product
    return total


def partial_kernel(starts, *refs):
    number = len(starts)
    total = refs[2 * number][...] if len(refs) == 2 * number + 2 else None
    for chunk_ref, store_ref, start in zip(refs, refs[number:], starts):
        total = products([chunk_ref], store_ref, start, total)
    refs[-1][...] = total


def partial_call(chunks, stores, starts, total=None):
    _, count, layers, width = stores[0].shape
    entries = sum(chunk.shape[0] for chunk in chunks)
    flops = 2 * entries * count * layers * width * LANES
    operands = [*chunks, *stores] + ([] if total is None else [total])
    return pl.pallas_call(
        functools.partial(partial_kernel, tuple(starts)),
        out_shape=jax.ShapeDtypeStruct((count * layers, LANES), jnp.float32),
        in_specs=[IN_VMEM] * len(operands),
        out_specs=IN_VMEM,
        cost_estimate=pl.CostEstimate(flops=0, bytes_accessed=0, transcendentals=0),
        compiler_params=PARAMS,
    )(*operands)


def score_kernel(queries, start, *refs):
    *chunk_refs, store_ref, before_ref, scale_ref, out_ref, total_ref = refs
    _, count, layers, width = store_ref.shape
    span = LANES // (width // LANES)
    total_ref[...] = products(chunk_refs, store_ref, start, before_ref[...])
    lane = lax.broadcasted_iota(jnp.int32, (count, LANES), 1)
    mixed = total_ref[pl.ds(0, count, layers)]
    for layer in range(1, layers):
        rows = total_ref[pl.ds(layer, count, layers)]
        mixed = jnp.where(lane % span // queries == layer, rows, mixed)
    turned = mixed.T
    result = turned[:queries]
    for first in range(queries, LANES, queries):
        result = result + turned[first : first + queries]
    out_ref[...] = result * scale_ref[...]


def score_call(chunks, store, start, total, scaling, queries):
    _, count, layers, _ = store.shape
    return pl.pallas_call(
        functools.partial(score_kernel, queries, start),
        out_shape=jax.ShapeDtypeStruct((queries, count), jnp.float32),
        in_specs=[IN_VMEM] * (len(chunks) + 3),
        out_specs=IN_VMEM,
        scratch_shapes=[pltpu.VMEM(total.shape, jnp.float32)],
        compiler_params=PARAMS,
    )(*chunks, store, total, scaling[None, :])


def fits(size, factors, store, inv_fisher):
    queries, layers, _, width = factors.shape
    _, rows, feats = inv_fisher.shape
    return (
        size >= 16
        and size & (size - 1) == 0
        and width == LANES
        and queries == 2
        and layers == 2
        and rows % LANES == 0
        and (rows // LANES) * layers * queries * size == LANES
        and store.shape[0] % LANES == 0
        and feats == rows * size
    )


def solution(mesh):
    size = mesh.shape["blk"]

    def local(factors, token_mask, store, inv_fisher, source_ids, source_weight):
        if not fits(size, factors, store, inv_fisher):
            return plain(factors, token_mask, store, inv_fisher, source_ids, source_weight)
        scaling = make_scaling(source_ids, source_weight)
        grads = grads_call(factors, token_mask)
        ready = {}

        def keep(name, value):
            ready[name] = value
            return value

        def load(name, parts, after):
            return keep(name, load_store(store, size, parts, after))

        homes = (
            ("own", "core"),
            ("one", "core_one"),
            ("last",),
            ("core_last",),
        )

        def home_of(name):
            return next(k for k, home in enumerate(homes) if name in home)

        def start_of(name):
            home = homes[home_of(name)]
            return sum(entry_count(other, size) for other in home[: home.index(name)])

        got = gather(
            grads,
            size,
            FIRST,
            lambda share: [keep("fisher", load_whole(inv_fisher, share))],
            lambda got: [load(0, homes[0], got["own"])],
            lambda got: [load(1, homes[1], got["one"])],
        )
        got["core_last"], ready[2] = lax.optimization_barrier(
            (got["core_last"], load(2, homes[2], got["last"]))
        )
        hidden = fisher_call(got, ready["fisher"], size)

        def add(got, *names):
            total = partial_call(
                [got[name] for name in names],
                [ready[home_of(name)] for name in names],
                [start_of(name) for name in names],
                ready.get("total"),
            )
            return keep("total", total)

        got = gather(
            hidden,
            size,
            SECOND,
            lambda share: [load(3, homes[3], share)],
            lambda got: [],
            lambda got: [add(got, "own", "core", "one")],
        )
        add(got, "core_one", "last")
        return score_call(
            [got["core_last"]], ready[3], start_of("core_last"),
            ready["total"], scaling, factors.shape[0] * size,
        )

    placed = (
        P(("groups", "blk"), None, None, None),
        P(("groups", "blk"), None),
        P(("groups", "blk"), None, None),
        P(None, "blk", None),
        P(("groups", "blk")),
        P(),
    )
    return jax.shard_map(
        local, mesh=mesh, in_specs=placed, out_specs=P("groups", "blk"), check_vma=False
    )
```

```python
import functools
import math

import jax
import jax.numpy as jnp
from jax import lax
from jax.experimental import pallas as pl
from jax.experimental.pallas import tpu as pltpu
from jax.sharding import PartitionSpec as P

LANES = 128
IN_VMEM = pl.BlockSpec(memory_space=pltpu.VMEM)
IN_HBM = pl.BlockSpec(memory_space=pltpu.HBM)
PARAMS = pltpu.CompilerParams(vmem_limit_bytes=16 * 2**20)


def make_grads(factors, token_mask):
    rank_size = factors.shape[3] // 2
    mask_values = token_mask.astype(jnp.float32)[:, None, :, None]
    left_side = factors[..., :rank_size].astype(jnp.float32) * mask_values
    right_side = factors[..., rank_size:].astype(jnp.float32)
    outer_sum = jnp.einsum("qlta,qltb->qlab", left_side, right_side)
    return outer_sum.reshape(outer_sum.shape[0], outer_sum.shape[1], rank_size * rank_size).astype(
        jnp.bfloat16
    )


def make_scaling(source_ids, source_weight):
    matches = (
        source_ids[:, None] == jnp.arange(source_weight.shape[0], dtype=jnp.int32)[None, :]
    ).astype(jnp.float32)
    return jnp.sum(matches * source_weight[None, :], axis=1)


def plain(factors, token_mask, store, inv_fisher, source_ids, source_weight):
    segment = lax.all_gather(make_grads(factors, token_mask), "blk", axis=0, tiled=True)
    products = [
        lax.dot_general(
            segment[:, layer_idx],
            inv_fisher[layer_idx],
            (((1,), (1,)), ((), ())),
            preferred_element_type=jnp.float32,
        )
        for layer_idx in range(inv_fisher.shape[0])
    ]
    hidden_cols = jnp.stack(products, axis=1).astype(jnp.bfloat16)
    hidden = lax.all_gather(hidden_cols, "blk", axis=2, tiled=True)
    raw_scores = lax.dot_general(
        hidden, store, (((1, 2), (1, 2)), ((), ())), preferred_element_type=jnp.float32
    )
    return raw_scores * make_scaling(source_ids, source_weight)[None, :]


def zeros_kernel(out_ref):
    out_ref[...] = jnp.zeros_like(out_ref)


def zeros_call(shape):
    return pl.pallas_call(
        zeros_kernel,
        out_shape=jax.ShapeDtypeStruct(shape, jnp.float32),
        out_specs=IN_VMEM,
        cost_estimate=pl.CostEstimate(flops=10**10, bytes_accessed=0, transcendentals=0),
        compiler_params=PARAMS,
    )()


def grads_kernel(factors_ref, mask_ref, zeros_ref, out_ref, outer_ref, flat_ref):
    queries, layers, _, width = factors_ref.shape
    rank = width // 2
    tiles = rank * rank // LANES
    for layer in range(layers):
        for query in range(queries):
            block = factors_ref[query, layer].astype(jnp.float32)
            left = block[:, :rank].T * mask_ref[query : query + 1].astype(jnp.float32)
            outer_ref[...] = zeros_ref[...] + jnp.dot(
                left.astype(jnp.bfloat16),
                block[:, rank:].astype(jnp.bfloat16),
                preferred_element_type=jnp.float32,
            )
            flat_ref[layer, pl.ds(query, tiles, queries)] = jnp.concatenate(
                [outer_ref[pl.ds(0, tiles, 2)], outer_ref[pl.ds(1, tiles, 2)]], axis=1
            )
    out_ref[...] = (
        flat_ref[...].astype(jnp.bfloat16).reshape(layers * tiles, queries, LANES)
    )


def grads_call(factors, token_mask):
    queries, layers, _, width = factors.shape
    rank = width // 2
    tiles = rank * rank // LANES
    return pl.pallas_call(
        grads_kernel,
        out_shape=jax.ShapeDtypeStruct((layers * tiles, queries, LANES), jnp.bfloat16),
        grid=(1,),
        in_specs=[
            pl.BlockSpec(factors.shape, lambda i: (0, 0, 0, 0)),
            pl.BlockSpec(token_mask.shape, lambda i: (0, 0)),
            IN_VMEM,
        ],
        out_specs=pl.BlockSpec((layers * tiles, queries, LANES), lambda i: (0, 0, 0)),
        scratch_shapes=[
            pltpu.VMEM((rank, rank), jnp.float32),
            pltpu.VMEM((layers, tiles * queries, LANES), jnp.float32),
        ],
        cost_estimate=pl.CostEstimate(flops=10**10, bytes_accessed=0, transcendentals=0),
        compiler_params=PARAMS,
    )(factors, token_mask, zeros_call((rank, rank)))


def load_kernel(size, names, source_ref, out_ref, sem):
    width = out_ref.shape[-1]
    places = owners(size, SECOND)
    for entry, owner in enumerate(sum([places[name] for name in names], [])):
        columns = pl.ds(pl.multiple_of(owner * width, width), width)
        pltpu.make_async_copy(source_ref.at[:, :, columns], out_ref.at[entry], sem).start()
    pltpu.make_async_copy(out_ref, out_ref, sem).wait()


def load_store(store, size, names, after):
    store, _ = lax.optimization_barrier((store, after))
    rows, layers, feats = store.shape
    entries = sum(entry_count(name, size) for name in names)
    shape = (entries, rows, layers, feats // size)
    return pl.pallas_call(
        functools.partial(load_kernel, size, names),
        out_shape=jax.ShapeDtypeStruct(shape, store.dtype),
        in_specs=[IN_HBM],
        out_specs=IN_VMEM,
        scratch_shapes=[pltpu.SemaphoreType.DMA],
        cost_estimate=pl.CostEstimate(
            flops=0, bytes_accessed=2 * math.prod(shape), transcendentals=0
        ),
        compiler_params=PARAMS,
    )(store)


def copy_kernel(source_ref, out_ref, sem):
    copy = pltpu.make_async_copy(source_ref, out_ref, sem)
    copy.start()
    copy.wait()


def load_whole(source, after):
    source, _ = lax.optimization_barrier((source, after))
    return pl.pallas_call(
        copy_kernel,
        out_shape=jax.ShapeDtypeStruct(source.shape, source.dtype),
        in_specs=[IN_HBM],
        out_specs=IN_VMEM,
        scratch_shapes=[pltpu.SemaphoreType.DMA],
        cost_estimate=pl.CostEstimate(
            flops=0, bytes_accessed=2 * source.size, transcendentals=0
        ),
        compiler_params=PARAMS,
    )(source)


def send(value, even, odd, size):
    pairs = [(i, i ^ (odd if i % 2 else even)) for i in range(size)]
    return lax.ppermute(value, "blk", pairs)


def far_steps(size):
    return [size >> k for k in range(1, size.bit_length()) if size >> k > 4]


def gather(chunk, size, plan, early, middle, late):
    flip, square, late_core = plan
    share = chunk[None]
    for step in far_steps(size):
        other = send(share, step ^ flip, step ^ flip, size)
        if step == size // 2:
            other, *_ = lax.optimization_barrier((other, *early(share)))
        share = jnp.concatenate([share, other], axis=0)
    one, two, three = (send(share, even, odd, size) for even, odd in square)
    got = {"own": share}
    if late_core:
        one, *_ = lax.optimization_barrier((one, *middle(got)))
        held, _ = lax.optimization_barrier((share, one))
        got["core"] = send(held, 1, 1, size)
    else:
        got["core"] = send(share, 1, 1, size)
        one, got["core"], *_ = lax.optimization_barrier((one, got["core"], *middle(got)))
    got.update(one=one, core_one=send(one, 1, 1, size))
    two, three, *_ = lax.optimization_barrier(
        (two, three, got["core"], got["core_one"], *late(got))
    )
    last = jnp.concatenate([two, three], axis=0)
    got.update(last=last, core_last=send(last, 1, 1, size))
    return got


def owners(size, plan):
    me = lax.axis_index("blk")
    core = me ^ 1
    is_odd = lax.rem(me, 2) == 1
    share = [0]
    for step in far_steps(size):
        share = share + [step ^ plan[0] ^ entry for entry in share]
    places = {"own": [me ^ entry for entry in share], "core": [core ^ entry for entry in share]}
    for name, (even, odd) in zip(("one", "two", "three"), plan[1]):
        if even % 2:
            even, odd = odd, even
        mine, theirs = jnp.where(is_odd, odd, even), jnp.where(is_odd, even, odd)
        places[name] = [me ^ mine ^ entry for entry in share]
        places["core_" + name] = [core ^ theirs ^ entry for entry in share]
    for name in ("", "core_"):
        places[name + "last"] = places.pop(name + "two") + places.pop(name + "three")
    return places


def entry_count(name, size):
    return (2 if name.endswith("last") else 1) << len(far_steps(size))


FIRST = (1, ((7, 7), (5, 5), (3, 3)), True)
SECOND = (1, ((7, 7), (5, 5), (3, 3)), False)
NAMES = ("own", "core", "one", "core_one", "last", "core_last")


def fisher_kernel(size, *refs):
    part_refs, (fisher_ref, out_ref, whole_ref) = refs[:-3], refs[-3:]
    layers, rows, feats = fisher_ref.shape
    tiles = feats // LANES
    queries = whole_ref.shape[2]
    places_of = owners(size, FIRST)
    for ref, name in zip(part_refs, NAMES):
        for entry, place in enumerate(places_of[name]):
            whole_ref[place] = ref[entry]
    parts = []
    for layer in range(layers):
        grads = jnp.concatenate(
            [
                whole_ref[:, layer * tiles + tile].reshape(size * queries, LANES)
                for tile in range(tiles)
            ],
            axis=1,
        )
        parts.append(
            lax.dot_general(
                fisher_ref[layer],
                grads,
                (((1,), (1,)), ((), ())),
                preferred_element_type=jnp.float32,
            )
        )
    pieces = [
        part[start : start + LANES] for start in range(0, rows, LANES) for part in parts
    ]
    out_ref[...] = jnp.concatenate(pieces, axis=1).astype(jnp.bfloat16)


def fisher_call(got, inv_fisher, size):
    chunk_shape = got["own"].shape[1:]
    return pl.pallas_call(
        functools.partial(fisher_kernel, size),
        out_shape=jax.ShapeDtypeStruct((LANES, LANES), jnp.bfloat16),
        in_specs=[IN_VMEM] * (len(NAMES) + 1),
        out_specs=IN_VMEM,
        scratch_shapes=[pltpu.VMEM((size,) + chunk_shape, jnp.bfloat16)],
        compiler_params=PARAMS,
    )(*[got[name] for name in NAMES], inv_fisher)


def products(chunk_refs, store_ref, start, total):
    _, count, layers, width = store_ref.shape
    groups = width // LANES
    span = LANES // groups
    lane = lax.broadcasted_iota(jnp.int32, (LANES, LANES), 1)
    for ref in chunk_refs:
        for entry in range(ref.shape[0]):
            chunk = ref[entry]
            weights = jnp.concatenate(
                [
                    jnp.where(lane // span == group, chunk, jnp.zeros_like(chunk))
                    for group in range(groups)
                ],
                axis=0,
            )
            rows = store_ref[start].reshape(count * layers, width)
            start += 1
            product = jnp.dot(rows, weights, preferred_element_type=jnp.float32)
            total = product if total is None else total + product
    return total


def partial_kernel(starts, *refs):
    number = len(starts)
    total = refs[2 * number][...] if len(refs) == 2 * number + 2 else None
    for chunk_ref, store_ref, start in zip(refs, refs[number:], starts):
        total = products([chunk_ref], store_ref, start, total)
    refs[-1][...] = total


def partial_call(chunks, stores, starts, total=None):
    _, count, layers, width = stores[0].shape
    entries = sum(chunk.shape[0] for chunk in chunks)
    flops = 2 * entries * count * layers * width * LANES
    operands = [*chunks, *stores] + ([] if total is None else [total])
    return pl.pallas_call(
        functools.partial(partial_kernel, tuple(starts)),
        out_shape=jax.ShapeDtypeStruct((count * layers, LANES), jnp.float32),
        in_specs=[IN_VMEM] * len(operands),
        out_specs=IN_VMEM,
        cost_estimate=pl.CostEstimate(flops=0, bytes_accessed=0, transcendentals=0),
        compiler_params=PARAMS,
    )(*operands)


def score_kernel(queries, start, *refs):
    *chunk_refs, store_ref, before_ref, scale_ref, out_ref, total_ref = refs
    _, count, layers, width = store_ref.shape
    span = LANES // (width // LANES)
    total_ref[...] = products(chunk_refs, store_ref, start, before_ref[...])
    lane = lax.broadcasted_iota(jnp.int32, (count, LANES), 1)
    mixed = total_ref[pl.ds(0, count, layers)]
    for layer in range(1, layers):
        rows = total_ref[pl.ds(layer, count, layers)]
        mixed = jnp.where(lane % span // queries == layer, rows, mixed)
    turned = mixed.T
    result = turned[:queries]
    for first in range(queries, LANES, queries):
        result = result + turned[first : first + queries]
    out_ref[...] = result * scale_ref[...]


def score_call(chunks, store, start, total, scaling, queries):
    _, count, layers, _ = store.shape
    return pl.pallas_call(
        functools.partial(score_kernel, queries, start),
        out_shape=jax.ShapeDtypeStruct((queries, count), jnp.float32),
        in_specs=[IN_VMEM] * (len(chunks) + 3),
        out_specs=IN_VMEM,
        scratch_shapes=[pltpu.VMEM(total.shape, jnp.float32)],
        compiler_params=PARAMS,
    )(*chunks, store, total, scaling[None, :])


def fits(size, factors, store, inv_fisher):
    queries, layers, _, width = factors.shape
    _, rows, feats = inv_fisher.shape
    return (
        size >= 16
        and size & (size - 1) == 0
        and width == LANES
        and queries == 2
        and layers == 2
        and rows % LANES == 0
        and (rows // LANES) * layers * queries * size == LANES
        and store.shape[0] % LANES == 0
        and feats == rows * size
    )


def solution(mesh):
    size = mesh.shape["blk"]

    def local(factors, token_mask, store, inv_fisher, source_ids, source_weight):
        if not fits(size, factors, store, inv_fisher):
            return plain(factors, token_mask, store, inv_fisher, source_ids, source_weight)
        scaling = make_scaling(source_ids, source_weight)
        grads = grads_call(factors, token_mask)
        ready = {}

        def keep(name, value):
            ready[name] = value
            return value

        def load(name, parts, after):
            return keep(name, load_store(store, size, parts, after))

        homes = (
            ("own", "core"),
            ("one", "core_one"),
            ("last",),
            ("core_last",),
        )

        def home_of(name):
            return next(k for k, home in enumerate(homes) if name in home)

        def start_of(name):
            home = homes[home_of(name)]
            return sum(entry_count(other, size) for other in home[: home.index(name)])

        got = gather(
            grads,
            size,
            FIRST,
            lambda share: [keep("fisher", load_whole(inv_fisher, share))],
            lambda got: [load(0, homes[0], got["own"])],
            lambda got: [],
        )
        got["core_last"], ready[1] = lax.optimization_barrier(
            (got["core_last"], load(1, homes[1], got["last"]))
        )
        hidden = fisher_call(got, ready["fisher"], size)

        def add(got, *names):
            total = partial_call(
                [got[name] for name in names],
                [ready[home_of(name)] for name in names],
                [start_of(name) for name in names],
                ready.get("total"),
            )
            return keep("total", total)

        got = gather(
            hidden,
            size,
            SECOND,
            lambda share: [load(2, homes[2], share)],
            lambda got: [add(got, "own", "core"), load(3, homes[3], got["core"])],
            lambda got: [add(got, "one")],
        )
        add(got, "core_one", "last")
        return score_call(
            [got["core_last"]], ready[3], start_of("core_last"),
            ready["total"], scaling, factors.shape[0] * size,
        )

    placed = (
        P(("groups", "blk"), None, None, None),
        P(("groups", "blk"), None),
        P(("groups", "blk"), None, None),
        P(None, "blk", None),
        P(("groups", "blk")),
        P(),
    )
    return jax.shard_map(
        local, mesh=mesh, in_specs=placed, out_specs=P("groups", "blk"), check_vma=False
    )
```
